512 devices in a mesh: blk: 32 (over z_hi, y, core), row: 16 (over x, z_lo).
Axes of the slice: x: 4, y: 8, z: 8 (z_hi: 2, z_lo: 4; z = z_hi * 4 + z_lo), core: 2. Of those that a mesh axis runs over, the one named last changes fastest.
Arguments:
- image: bfloat16 [49152, 1152], P(('blk', 'row')), may hold values from -0.1796875 to 0.1796875
- text: bfloat16 [49152, 1152], P(('blk', 'row')), may hold values from -0.1796875 to 0.1796875
- positive: int32 [49152], P(('blk', 'row')), may hold values from 0 to 1535
- plan: int32 [2, 32], replicated, may hold values from 0 to 31, as said below
- logit_scale: float32 [1], replicated, may hold values from 4 to 16
- logit_bias: float32 [1], replicated, may hold values from -4 to -1.5
Outputs:
- grad_image: bfloat16 [49152, 1152], P(('blk', 'row'))
- grad_text: bfloat16 [49152, 1152], P(('blk', 'row'))
The draws below stay inside these ranges and needn't reach their ends.
Inputs may be any that keep to these rules, and one draw needn't show every extreme that they name: plan[k, i] = i XOR m_k, where the 2 masks m_k are distinct and nonzero.
All inputs are finite; a program needn't handle non-finite values.
Results may differ from the reference program's by a relative error of at most 0.025.
Values may be sent and summed in bfloat16 or wider, within the bound.
A program may use at most 64 MiB of HBM per device.

```python
import math
import jax
import jax.numpy as jnp
from jax import lax

D = 1152
ROWS = 96
ROUNDS = 2
BLOCK = 1536
BATCH = 49152
N_BLK = 32
N_ROW = 16


def draw_plan(key, part):
    key = jax.random.fold_in(key, 11)
    masks = (jax.random.permutation(key, N_BLK - 1)[:ROUNDS] + 1).astype(jnp.int32)
    blocks = jnp.arange(N_BLK, dtype=jnp.int32)
    return jnp.bitwise_xor(blocks[None, :], masks[:, None])


def touch_ends(result, key, least, high):
    extent = result.shape
    spot = [jax.random.randint(jax.random.fold_in(key, axis), (), 0, extent[axis]) for axis in range(len(extent))]
    result = result.at[tuple(spot)].set(least)
    longest = extent.index(max(extent))
    spot[longest] = (spot[longest] + 1) % extent[longest]
    return result.at[tuple(spot)].set(high)


def shard_levels(key, dims, shards, least, top_value):
    def one(dim, blocks):
        steps = jax.random.uniform(jax.random.fold_in(jax.random.fold_in(key, 6), dim), (blocks,), jnp.float32, least / len(shards), top_value / len(shards))
        return jnp.repeat(jnp.exp(steps), dims[dim] // blocks).reshape((-1,) + (1,) * (len(dims) - dim - 1))

    factor_of = one(*shards[0])
    for cut in shards[1:]:
        factor_of = factor_of * one(*cut)
    return factor_of


def scatter_about(key, dims, deviation, reach, shards=(), kind=jnp.bfloat16):
    entries = jax.random.normal(key, dims, jnp.float32) * deviation
    if len(shards) > 0:
        entries = shard_levels(key, dims, shards, -0.22, 0.18) * entries
    return jnp.clip(entries, min=-reach, max=reach).astype(kind)


def setup_inputs(seed: int = 0) -> dict:
    key_of = jax.random.split(jax.random.key(seed), 7)
    return {
        "image": scatter_about(key_of[0], (BATCH, D), 0.03, 0.1796875, ((0, 512),)),
        "text": scatter_about(key_of[1], (BATCH, D), 0.03, 0.1796875, ((0, 512),)),
        "positive": touch_ends(jax.random.randint(key_of[2], (BATCH,), 0, BLOCK), jax.random.fold_in(key_of[2], 1), 0, BLOCK - 1).astype(jnp.int32),
        "plan": draw_plan(jax.random.fold_in(key_of[6], 71), 0),
        "logit_scale": jnp.clip(jnp.exp(jax.random.uniform(key_of[4], (1,), jnp.float32, math.log(4.0), math.log(16.0))), 4.0, 16.0),
        "logit_bias": jnp.clip(jax.random.uniform(key_of[5], (1,), jnp.float32, -4.0, -1.5), -4.0, -1.5),
    }


def unit_rows(x):
    xf = x.astype(jnp.float32)
    norm = jnp.sqrt(lax.optimization_barrier(jnp.sum(xf * xf, axis=-1, keepdims=True)) + 1e-06)
    return (xf / norm, norm)

def norm_backward(grad, unit, norm):
    return (grad - unit * lax.optimization_barrier(jnp.sum(unit * grad, axis=-1, keepdims=True))) / norm

def logits(left, right, scale, bias):
    prod = lax.dot_general(left, right, (((1,), (1,)), ((), ())), preferred_element_type=jnp.float32)
    return scale * prod + bias

def reference(image, text, positive, plan, logit_scale, logit_bias):
    img_unit, img_norm = unit_rows(image)
    txt_unit, txt_norm = unit_rows(text)
    img_blocks = img_unit.astype(jnp.bfloat16).reshape(N_BLK, BLOCK, D)
    txt_blocks = txt_unit.astype(jnp.bfloat16).reshape(N_BLK, BLOCK, D)
    pos_blocks = positive.reshape(N_BLK, BLOCK)
    scale = logit_scale[0]
    bias = logit_bias[0]
    columns = jnp.arange(BLOCK, dtype=jnp.int32)

    def per_block(index):
        own_img = img_blocks[index]
        own_txt = txt_blocks[index]
        labels = jnp.where(columns[None, :] == pos_blocks[index][:, None], 1.0, -1.0).astype(jnp.float32)
        self_scores = logits(own_img, own_txt, scale, bias)
        self_grad = (-labels * jax.nn.sigmoid(-labels * self_scores)).astype(jnp.bfloat16)
        img_grad = scale * jnp.dot(self_grad, own_txt, preferred_element_type=jnp.float32)
        partial_value = jnp.einsum('rab,rad->rbd', self_grad.astype(jnp.float32).reshape(N_ROW, ROWS, BLOCK), own_img.astype(jnp.float32).reshape(N_ROW, ROWS, D))
        for step in range(ROUNDS):
            other = plan[step, index]
            other_txt = txt_blocks[other]
            other_img = img_blocks[other]
            weights = jax.nn.sigmoid(logits(own_img, other_txt, scale, bias)).astype(jnp.bfloat16)
            term = (scale * jnp.dot(weights, other_txt, preferred_element_type=jnp.float32)).astype(jnp.bfloat16)
            term = lax.optimization_barrier(term)
            img_grad = img_grad + term.astype(jnp.float32)
            mirror = jax.nn.sigmoid(logits(other_img, own_txt, scale, bias)).astype(jnp.bfloat16)
            partial_value = partial_value + jnp.einsum('rab,rad->rbd', mirror.astype(jnp.float32).reshape(N_ROW, ROWS, BLOCK), other_img.astype(jnp.float32).reshape(N_ROW, ROWS, D))
        rounded = lax.optimization_barrier(partial_value.astype(jnp.bfloat16))
        txt_grad = scale * lax.optimization_barrier(jnp.sum(rounded.astype(jnp.float32), axis=0))
        return (img_grad, txt_grad)
    img_grads, txt_grads = lax.map(per_block, jnp.arange(N_BLK, dtype=jnp.int32))
    img_grads = img_grads.reshape(BATCH, D)
    txt_grads = txt_grads.reshape(BATCH, D)
    grad_image = norm_backward(img_grads, img_unit, img_norm).astype(jnp.bfloat16)
    grad_text = norm_backward(txt_grads, txt_unit, txt_norm).astype(jnp.bfloat16)
    return (grad_image, grad_text)
```

```python
import jax
import jax.numpy as jnp
from jax import lax
from jax.sharding import PartitionSpec as P


def exchange(value, mask):
    count = lax.axis_size("blk")

    def branch(m):
        pairs = [(source, source ^ m) for source in range(count)]
        return lambda v: lax.ppermute(v, "blk", pairs)

    return lax.switch(mask - 1, [branch(m) for m in range(1, count)], value)


def unit_rows(x):
    xf = x.astype(jnp.float32)
    norm = jnp.sqrt(jnp.sum(xf * xf, axis=-1, keepdims=True) + 1e-06)
    return (xf / norm, norm)


def norm_backward(grad, unit, norm):
    return (grad - unit * jnp.sum(unit * grad, axis=-1, keepdims=True)) / norm


def logits(left, right, scale, bias):
    prod = lax.dot_general(
        left, right, (((1,), (1,)), ((), ())), preferred_element_type=jnp.float32
    )
    return scale * prod + bias


def shards(image, text, positive, plan, logit_scale, logit_bias):
    scale = logit_scale[0]
    bias = logit_bias[0]
    img_unit, img_norm = unit_rows(image)
    txt_unit, txt_norm = unit_rows(text)
    img_hat = img_unit.astype(jnp.bfloat16)
    txt_hat = txt_unit.astype(jnp.bfloat16)
    text_block = lax.all_gather(txt_hat, "row", axis=0, tiled=True)
    columns = jnp.arange(text_block.shape[0], dtype=jnp.int32)
    labels = jnp.where(columns[None, :] == positive[:, None], 1.0, -1.0).astype(jnp.float32)
    self_scores = logits(img_hat, text_block, scale, bias)
    self_grad = (-labels * jax.nn.sigmoid(-labels * self_scores)).astype(jnp.bfloat16)
    img_grad = scale * jnp.dot(self_grad, text_block, preferred_element_type=jnp.float32)
    masks = plan[:, 0]
    rounds = plan.shape[0]
    lefts = [img_hat]
    grads = [self_grad]
    returned_list = []
    for step in range(rounds):
        flat = exchange(img_hat, masks[step])
        weights = jax.nn.sigmoid(logits(flat, text_block, scale, bias)).astype(jnp.bfloat16)
        back = (scale * jnp.dot(weights, text_block, preferred_element_type=jnp.float32)).astype(
            jnp.bfloat16
        )
        returned_list.append(exchange(back, masks[step]))
        lefts.append(flat)
        grads.append(weights)
    for term in returned_list:
        img_grad = img_grad + term.astype(jnp.float32)
    left_all = jnp.concatenate(lefts, axis=0)
    grad_all = jnp.concatenate(grads, axis=0)
    partial_value = lax.dot_general(
        grad_all, left_all, (((0,), (0,)), ((), ())), preferred_element_type=jnp.float32
    )
    summed = lax.psum_scatter(
        partial_value.astype(jnp.bfloat16), "row", scatter_dimension=0, tiled=True
    ).astype(jnp.float32)
    txt_grad = scale * summed
    grad_image = norm_backward(img_grad, img_unit, img_norm).astype(jnp.bfloat16)
    grad_text = norm_backward(txt_grad, txt_unit, txt_norm).astype(jnp.bfloat16)
    return (grad_image, grad_text)


def solution(mesh):
    placed = (P(("blk", "row"), None), P(("blk", "row"), None), P(("blk", "row")), P(), P(), P())
    return jax.shard_map(
        shards,
        mesh=mesh,
        in_specs=placed,
        out_specs=(P(("blk", "row"), None), P(("blk", "row"), None)),
        check_vma=False,
    )
```

```python
import jax
import jax.numpy as jnp
from jax import lax
from jax.experimental import pallas as pl
from jax.experimental.pallas import tpu as pltpu
from jax.sharding import PartitionSpec as P

MESH = pl.DeviceIdType.MESH
VMEM = pl.BlockSpec(memory_space=pltpu.VMEM)
SMEM = pl.BlockSpec(memory_space=pltpu.SMEM)
SIDE = 4
ROWS = 96
HALF = 48
TILE = SIDE * ROWS
WIDTH = 1152


def place():
    row = lax.axis_index("row")
    return lax.div(row, SIDE), lax.rem(row, SIDE)


def device(x, z):
    return {"row": lax.rem(x, SIDE) * SIDE + z}


def remote(src, dst, send, recv, index, target):
    return pltpu.make_async_remote_copy(
        src_ref=src,
        dst_ref=dst,
        send_sem=send.at[index],
        recv_sem=recv.at[index],
        device_id=target,
        device_id_type=MESH,
    )


def greet(ring, chain):
    x, z = place()
    barrier = pltpu.get_barrier_semaphore()

    def signal(target):
        pl.semaphore_signal(barrier, inc=1, device_id=target, device_id_type=MESH)

    count = ring
    for offset in (1, 2, 3) if ring == 3 else (1, 3):
        signal(device(x + offset, z))
    if chain:
        count = ring + jnp.where(z < SIDE - 1, 1, 0) + jnp.where(z > 0, 1, 0)

        @pl.when(z < SIDE - 1)
        def _():
            signal(device(x, z + 1))

        @pl.when(z > 0)
        def _():
            signal(device(x, z - 1))

    pl.semaphore_wait(barrier, count)


LO = pl.ds(0, HALF)
HI = pl.ds(HALF, HALF)


class RingGather:
    copies = 6

    def __init__(self, src, dst, send, recv, base):
        x, z = place()
        after, before = lax.rem(x + 1, SIDE), lax.rem(x + 3, SIDE)
        up, down = device(after, z), device(before, z)

        def copy(source, slot, part, index, target):
            return remote(source.at[part], dst.at[slot, part], send, recv, base + index, target)

        self.first = [
            copy(src, x, LO, 0, up),
            copy(src, x, HI, 1, down),
            copy(src, x, HI, 2, up),
            copy(src, x, LO, 3, down),
        ]
        self.onward = [
            copy(dst.at[before], before, LO, 4, up),
            copy(dst.at[after], after, HI, 5, down),
        ]

    def start(self):
        for copy in self.first:
            copy.start()

    def forward(self):
        for first, onward in zip(self.first, self.onward):
            first.wait_recv()
            onward.start()

    def finish(self):
        for copy in self.first[2:] + self.onward:
            copy.wait_recv()
        for copy in self.first + self.onward:
            copy.wait_send()


class ChainGather:
    copies = 6

    def __init__(self, src, dst, send, recv, base):
        self.refs = (src, dst, send, recv, base)
        self.x, self.z = place()

    def copy(self, step, sign):
        src, dst, send, recv, base = self.refs
        slot = self.z - sign * step
        index = base + step + (0 if sign > 0 else 3)
        source = src if step == 0 else dst.at[slot]
        return remote(source, dst.at[slot], send, recv, index, device(self.x, self.z + sign))

    def sends(self, step, sign):
        first = self.z - sign * step
        inside = (first >= 0) & (first < SIDE)
        return inside & ((self.z < SIDE - 1) if sign > 0 else (self.z > 0))

    def gets(self, step, sign):
        first = self.z - sign * (step + 1)
        return (first >= 0) & (first < SIDE)

    def start(self):
        for sign in (1, -1):

            @pl.when(self.sends(0, sign))
            def _():
                self.copy(0, sign).start()

    def step(self, step):
        for sign in (1, -1):

            @pl.when(self.gets(step, sign))
            def _():
                self.copy(step, sign).wait_recv()

            if step < SIDE - 2:

                @pl.when(self.sends(step + 1, sign))
                def _():
                    self.copy(step + 1, sign).start()

    def finish(self):
        for step in range(SIDE - 1):
            for sign in (1, -1):

                @pl.when(self.sends(step, sign))
                def _():
                    self.copy(step, sign).wait_send()


def add(*terms):
    total = terms[0].astype(jnp.float32)
    for term in terms[1:]:
        total = total + term.astype(jnp.float32)
    return total


class RingSum:
    copies = 6

    def __init__(self, part, relay, out, inbox, send, recv, base):
        x, z = place()
        self.x = x
        self.after, self.before, across = (lax.rem(x + k, SIDE) for k in (1, 3, 2))
        up, down = device(self.after, z), device(self.before, z)
        self.part, self.relay, self.out, self.inbox = part, relay, out, inbox
        self.first = [
            remote(part.at[across, LO], relay.at[0], send, recv, base, up),
            remote(part.at[across, HI], relay.at[1], send, recv, base + 1, down),
            remote(part.at[self.after, HI], inbox.at[0, HI], send, recv, base + 2, up),
            remote(part.at[self.before, LO], inbox.at[1, LO], send, recv, base + 3, down),
        ]
        self.onward = [
            remote(out.at[0], inbox.at[0, LO], send, recv, base + 4, up),
            remote(out.at[1], inbox.at[1, HI], send, recv, base + 5, down),
        ]

    def start(self):
        for copy in self.first:
            copy.start()

    def forward(self):
        self.first[0].wait_recv()
        self.out[0] = add(self.part[self.after, LO], self.relay[0]).astype(jnp.bfloat16)
        self.onward[0].start()
        self.first[1].wait_recv()
        self.out[1] = add(self.part[self.before, HI], self.relay[1]).astype(jnp.bfloat16)
        self.onward[1].start()

    def finish(self):
        for copy in self.first[2:] + self.onward:
            copy.wait_recv()
        for copy in self.first + self.onward:
            copy.wait_send()
        return add(self.part[self.x], self.inbox[0], self.inbox[1])


RING_SUM = [
    pltpu.VMEM((2, HALF, WIDTH), jnp.bfloat16),
    pltpu.VMEM((2, HALF, WIDTH), jnp.bfloat16),
    pltpu.VMEM((2, ROWS, WIDTH), jnp.bfloat16),
]


class ChainSum:
    copies = 6

    def __init__(self, part, out, inbox, send, recv, base):
        self.refs = (part, out, inbox, send, recv, base)
        self.x, self.z = place()

    def copy(self, step, sign):
        part, out, inbox, send, recv, base = self.refs
        lane = 0 if sign > 0 else 1
        return remote(
            out.at[lane, step],
            inbox.at[lane, step],
            send,
            recv,
            base + step + 3 * lane,
            device(self.x, self.z + sign),
        )

    def slot(self, step, sign):
        return SIDE - 1 - step if sign > 0 else step

    def sends(self, step, sign):
        slot = self.slot(step, sign)
        return self.z < slot if sign > 0 else self.z > slot

    def fed(self, sign):
        return self.z > 0 if sign > 0 else self.z < SIDE - 1

    def step(self, step):
        part, out, inbox = self.refs[:3]
        for sign in (1, -1):
            lane = 0 if sign > 0 else 1
            slot = self.slot(step, sign)

            @pl.when(self.sends(step, sign) & self.fed(sign))
            def _():
                self.copy(step, sign).wait_recv()
                out[lane, step] = add(part[slot], inbox[lane, step]).astype(jnp.bfloat16)
                self.copy(step, sign).start()

            @pl.when(self.sends(step, sign) & jnp.logical_not(self.fed(sign)))
            def _():
                out[lane, step] = part[slot]
                self.copy(step, sign).start()

    def finish(self, total):
        part, out, inbox = self.refs[:3]
        total[...] = part[self.z].astype(jnp.float32)
        for step in range(SIDE - 1):
            for sign in (1, -1):
                lane = 0 if sign > 0 else 1

                @pl.when(self.z == self.slot(step, sign))
                def _():
                    self.copy(step, sign).wait_recv()
                    total[...] += inbox[lane, step].astype(jnp.float32)

                @pl.when(self.sends(step, sign))
                def _():
                    self.copy(step, sign).wait_send()


CHAIN_SUM = [
    pltpu.VMEM((2, SIDE - 1, ROWS, WIDTH), jnp.bfloat16),
    pltpu.VMEM((2, SIDE - 1, ROWS, WIDTH), jnp.bfloat16),
]


def semaphores(count):
    return [pltpu.SemaphoreType.DMA((count,)), pltpu.SemaphoreType.DMA((count,))]


def call(kernel, name, number, out, scratch, flops=0, specs=None):
    def run(*args):
        return pl.pallas_call(
            kernel,
            out_shape=out,
            in_specs=specs or [VMEM] * len(args),
            out_specs=jax.tree.map(lambda _: VMEM, out),
            scratch_shapes=scratch,
            compiler_params=pltpu.CompilerParams(
                collective_id=number, has_side_effects=True, vmem_limit_bytes=48 * 2**20
            ),
            cost_estimate=pl.CostEstimate(flops=flops, bytes_accessed=2**25, transcendentals=0),
            name=name,
        )(*args)

    return run


def bf16(*shape):
    return jax.ShapeDtypeStruct(shape, jnp.bfloat16)


def gather_own(image, text, positive, images, texts, places, send, recv):
    x, z = place()
    greet(3, True)
    chain = ChainGather(text, texts, send, recv, 0)
    ring = RingGather(image, images, send, recv, 6)
    hints = [
        remote(positive, places.at[x], send, recv, 12 + k, device(x + k, z)) for k in (1, 2, 3)
    ]
    chain.start()
    ring.start()
    for hint in hints:
        hint.start()
    texts[z] = text[...]
    images[x] = image[...]
    places[x] = positive[...]
    ring.forward()
    for step in range(SIDE - 1):
        chain.step(step)
    ring.finish()
    chain.finish()
    for hint in hints:
        hint.wait()


def gather_ring(image, images, send, recv):
    x, _ = place()
    greet(2, False)
    ring = RingGather(image, images, send, recv, 0)
    ring.start()
    images[x] = image[...]
    ring.forward()
    ring.finish()


def weights(images, texts, scale, bias):
    prod = lax.dot_general(
        images, texts, (((1,), (1,)), ((), ())), preferred_element_type=jnp.float32
    )
    return 0.5 * jnp.tanh(0.5 * (scale * prod + bias)) + 0.5


def products(images, texts, grad, scale, part, total, first):
    texts_whole = texts[...].reshape(TILE, WIDTH)
    images_whole = images[...].reshape(TILE, WIDTH)
    back = scale * jnp.dot(grad, texts_whole, preferred_element_type=jnp.float32)
    part[...] = back.astype(jnp.bfloat16).reshape(SIDE, ROWS, WIDTH)
    gain = lax.dot_general(
        grad, images_whole, (((0,), (0,)), ((), ())), preferred_element_type=jnp.float32
    )
    if first:
        total[...] = gain
    else:
        total[...] += gain


def middle(
    scalars,
    texts,
    own,
    one,
    fetched,
    places,
    back_one,
    part_own,
    part_two,
    part_text,
    two,
    part_one,
    total,
    relay,
    out,
    inbox,
    send,
    recv,
):
    x, _ = place()
    scale = scalars[0]
    bias = scalars[1]
    greet(2, False)
    ring = RingGather(fetched, two, send, recv, 0)
    ring.start()
    two[x] = fetched[...]

    def grads(images):
        flat = images[...].reshape(TILE, WIDTH)
        return weights(flat, texts[...].reshape(TILE, WIDTH), scale, bias)

    products(one, texts, grads(one).astype(jnp.bfloat16), scale, part_one, total, True)
    sums = RingSum(part_one, relay, out, inbox, send, recv, 6)
    sums.start()
    ring.forward()

    columns = lax.broadcasted_iota(jnp.int32, (ROWS, TILE), 1) + x * TILE
    marks = []
    for slot in range(SIDE):
        spread = jnp.broadcast_to(places[slot, 0:1, :], (128, 128)).T
        marks.append(columns == spread[:ROWS, 0:1])
    mark = jnp.concatenate([jnp.where(m, 1.0, 0.0) for m in marks], axis=0)
    products(own, texts, (grads(own) - mark).astype(jnp.bfloat16), scale, part_own, total, False)
    sums.forward()
    ring.finish()
    products(two, texts, grads(two).astype(jnp.bfloat16), scale, part_two, total, False)
    part_text[...] = total[...].astype(jnp.bfloat16).reshape(SIDE, ROWS, WIDTH)
    back_one[...] = sums.finish().astype(jnp.bfloat16)


def sum_both(part, part_text, back, total, relay, out, inbox, chain_out, chain_in, send, recv):
    greet(2, True)
    sums = RingSum(part, relay, out, inbox, send, recv, 0)
    chain = ChainSum(part_text, chain_out, chain_in, send, recv, 6)
    sums.start()
    chain.step(0)
    sums.forward()
    chain.step(1)
    chain.step(2)
    back[...] = sums.finish().astype(jnp.bfloat16)
    chain.finish(total)


def sum_ring(part, total, relay, out, inbox, send, recv):
    greet(2, False)
    sums = RingSum(part, relay, out, inbox, send, recv, 0)
    sums.start()
    sums.forward()
    total[...] = sums.finish()


def exchange(value, mask, beside):
    count = lax.axis_size("blk")

    def branch(m):
        pairs = [(source, source ^ m) for source in range(count)]

        def run(value, *args):
            return lax.ppermute(value, "blk", pairs), beside(*args)

        return run

    branches = [branch(m) for m in range(1, count)]
    return lambda *args: lax.switch(mask - 1, branches, value, *args)


def unit_rows(x):
    xf = x.astype(jnp.float32)
    norm = jnp.sqrt(jnp.sum(xf * xf, axis=-1, keepdims=True) + 1e-06)
    return (xf / norm, norm)


def norm_backward(grad, unit, norm):
    return (grad - unit * jnp.sum(unit * grad, axis=-1, keepdims=True)) / norm


def shards(image, text, positive, plan, logit_scale, logit_bias):
    scale = logit_scale[0]
    img_unit, img_norm = unit_rows(image)
    txt_unit, txt_norm = unit_rows(text)
    img_hat = img_unit.astype(jnp.bfloat16)
    txt_hat = txt_unit.astype(jnp.bfloat16)
    spots = jnp.broadcast_to(jnp.pad(positive, (0, 128 - ROWS))[None], (8, 128))
    masks = plan[:, 0]
    scalars = jnp.concatenate([logit_scale, logit_bias])
    stack = bf16(SIDE, ROWS, WIDTH)
    shard = bf16(ROWS, WIDTH)
    wide = jax.ShapeDtypeStruct((ROWS, WIDTH), jnp.float32)
    spread = jax.ShapeDtypeStruct((SIDE, 8, 128), jnp.int32)

    first = call(gather_own, "gather_own", 0, (stack, stack, spread), semaphores(16))
    fetched_one, (own, texts, places) = exchange(img_hat, masks[0], first)(img_hat, txt_hat, spots)
    second = call(gather_ring, "gather_ring", 1, stack, semaphores(6))
    fetched_two, one = exchange(img_hat, masks[1], second)(fetched_one)
    third = call(
        middle,
        "middle",
        2,
        (shard, stack, stack, stack),
        [
            pltpu.VMEM((SIDE, ROWS, WIDTH), jnp.bfloat16),
            pltpu.VMEM((SIDE, ROWS, WIDTH), jnp.bfloat16),
            pltpu.VMEM((TILE, WIDTH), jnp.float32),
            *RING_SUM,
            *semaphores(12),
        ],
        flops=18 * TILE * TILE * WIDTH,
        specs=[SMEM] + [VMEM] * 5,
    )
    back_one, part_own, part_two, part_text = third(scalars, texts, own, one, fetched_two, places)
    fourth = call(
        sum_both, "sum_both", 3, (shard, wide), [*RING_SUM, *CHAIN_SUM, *semaphores(12)]
    )
    returned_one, (back_two, txt_sum) = exchange(back_one, masks[0], fourth)(part_two, part_text)
    fifth = call(sum_ring, "sum_ring", 4, wide, [*RING_SUM, *semaphores(6)])
    returned_two, img_sum = exchange(back_two, masks[1], fifth)(part_own)
    img_grad = img_sum + returned_one.astype(jnp.float32) + returned_two.astype(jnp.float32)
    grad_image = norm_backward(img_grad, img_unit, img_norm).astype(jnp.bfloat16)
    grad_text = norm_backward(scale * txt_sum, txt_unit, txt_norm).astype(jnp.bfloat16)
    return (grad_image, grad_text)


def solution(mesh):
    placed = (P(("blk", "row"), None), P(("blk", "row"), None), P(("blk", "row")), P(), P(), P())
    return jax.shard_map(
        shards,
        mesh=mesh,
        in_specs=placed,
        out_specs=(P(("blk", "row"), None), P(("blk", "row"), None)),
        check_vma=False,
    )
```

```python
import jax
import jax.numpy as jnp
from jax import lax
from jax.experimental import pallas as pl
from jax.experimental.pallas import tpu as pltpu
from jax.sharding import PartitionSpec as P

MESH = pl.DeviceIdType.MESH
VMEM = pl.BlockSpec(memory_space=pltpu.VMEM)
SMEM = pl.BlockSpec(memory_space=pltpu.SMEM)
SIDE = 4
ROWS = 96
HALF = 48
TILE = SIDE * ROWS
WIDTH = 1152


def place():
    row = lax.axis_index("row")
    return lax.div(row, SIDE), lax.rem(row, SIDE)


def device(x, z):
    return {"row": lax.rem(x, SIDE) * SIDE + z}


def remote(src, dst, send, recv, index, target):
    return pltpu.make_async_remote_copy(
        src_ref=src,
        dst_ref=dst,
        send_sem=send.at[index],
        recv_sem=recv.at[index],
        device_id=target,
        device_id_type=MESH,
    )


def greet(ring, chain):
    x, z = place()
    barrier = pltpu.get_barrier_semaphore()

    def signal(target):
        pl.semaphore_signal(barrier, inc=1, device_id=target, device_id_type=MESH)

    count = ring
    for offset in (1, 2, 3) if ring == 3 else (1, 3):
        signal(device(x + offset, z))
    if chain:
        count = ring + jnp.where(z < SIDE - 1, 1, 0) + jnp.where(z > 0, 1, 0)

        @pl.when(z < SIDE - 1)
        def _():
            signal(device(x, z + 1))

        @pl.when(z > 0)
        def _():
            signal(device(x, z - 1))

    pl.semaphore_wait(barrier, count)


LO = pl.ds(0, HALF)
HI = pl.ds(HALF, HALF)


class RingGather:
    copies = 6

    def __init__(self, src, dst, send, recv, base):
        x, z = place()
        after, before = lax.rem(x + 1, SIDE), lax.rem(x + 3, SIDE)
        up, down = device(after, z), device(before, z)

        def copy(source, slot, part, index, target):
            return remote(source.at[part], dst.at[slot, part], send, recv, base + index, target)

        self.first = [
            copy(src, x, LO, 0, up),
            copy(src, x, HI, 1, down),
            copy(src, x, HI, 2, up),
            copy(src, x, LO, 3, down),
        ]
        self.onward = [
            copy(dst.at[before], before, LO, 4, up),
            copy(dst.at[after], after, HI, 5, down),
        ]

    def start(self):
        for copy in self.first:
            copy.start()

    def forward(self):
        for first, onward in zip(self.first, self.onward):
            first.wait_recv()
            onward.start()

    def finish(self):
        for copy in self.first[2:] + self.onward:
            copy.wait_recv()
        for copy in self.first + self.onward:
            copy.wait_send()


class ChainGather:
    def __init__(self, src, dst, send, recv, base):
        self.refs = (src, dst, send, recv, base)
        self.x, self.z = place()

    def copy(self, step, lane, own=False):
        src, dst, send, recv, base = self.refs
        sign = 1 - 2 * lane
        slot = self.z - sign * step
        source = src if own else dst.at[slot]
        target = device(self.x, self.z + sign)
        return remote(source, dst.at[slot], send, recv, base + step + 3 * lane, target)

    def sends(self, step, lane):
        edge = self.z + 1 - 2 * lane
        first = self.z - (1 - 2 * lane) * step
        return (first >= 0) & (first < SIDE) & (edge >= 0) & (edge < SIDE) & (step < SIDE - 1)

    def gets(self, step, lane):
        first = self.z - (1 - 2 * lane) * (step + 1)
        return (first >= 0) & (first < SIDE)

    def start(self):
        @pl.loop(0, 2)
        def _(lane):
            @pl.when(self.sends(0, lane))
            def _():
                self.copy(0, lane, True).start()

    def forward(self):
        @pl.loop(0, 2 * (SIDE - 1))
        def _(i):
            step, lane = lax.div(i, 2), lax.rem(i, 2)

            @pl.when(self.gets(step, lane))
            def _():
                self.copy(step, lane).wait_recv()

            @pl.when(self.sends(step + 1, lane))
            def _():
                self.copy(step + 1, lane).start()

    def finish(self):
        @pl.loop(0, 2 * (SIDE - 1))
        def _(i):
            step, lane = lax.div(i, 2), lax.rem(i, 2)

            @pl.when(self.sends(step, lane))
            def _():
                self.copy(step, lane).wait_send()


def add(out, *terms):
    @pl.loop(0, out.shape[0] // 16)
    def _(i):
        rows = pl.ds(pl.multiple_of(i * 16, 16), 16)
        total = terms[0][rows].astype(jnp.float32)
        for term in terms[1:]:
            total = total + term[rows].astype(jnp.float32)
        out[rows] = total.astype(out.dtype)


class RingSum:
    def __init__(self, part, relay, out, inbox, send, recv, base):
        x, z = place()
        self.x = x
        self.after, self.before, across = (lax.rem(x + k, SIDE) for k in (1, 3, 2))
        up, down = device(self.after, z), device(self.before, z)
        self.part, self.relay, self.out, self.inbox = part, relay, out, inbox
        self.first = [
            remote(part.at[across, LO], relay.at[0], send, recv, base, up),
            remote(part.at[across, HI], relay.at[1], send, recv, base + 1, down),
            remote(part.at[self.after, HI], inbox.at[0, HI], send, recv, base + 2, up),
            remote(part.at[self.before, LO], inbox.at[1, LO], send, recv, base + 3, down),
        ]
        self.onward = [
            remote(out.at[0], inbox.at[0, LO], send, recv, base + 4, up),
            remote(out.at[1], inbox.at[1, HI], send, recv, base + 5, down),
        ]

    def start(self):
        for copy in self.first:
            copy.start()

    def forward(self):
        self.first[0].wait_recv()
        add(self.out.at[0], self.part.at[self.after, LO], self.relay.at[0])
        self.onward[0].start()
        self.first[1].wait_recv()
        add(self.out.at[1], self.part.at[self.before, HI], self.relay.at[1])
        self.onward[1].start()

    def finish(self, total):
        for copy in self.first[2:] + self.onward:
            copy.wait_recv()
        for copy in self.first + self.onward:
            copy.wait_send()
        add(total, self.part.at[self.x], self.inbox.at[0], self.inbox.at[1])


RING_SUM = [
    pltpu.VMEM((2, HALF, WIDTH), jnp.bfloat16),
    pltpu.VMEM((2, HALF, WIDTH), jnp.bfloat16),
    pltpu.VMEM((2, ROWS, WIDTH), jnp.bfloat16),
]


class ChainSum:
    def __init__(self, part, out, inbox, send, recv, base):
        self.refs = (part, out, inbox, send, recv, base)
        self.x, self.z = place()

    def copy(self, step, lane, own=False):
        part, out, inbox, send, recv, base = self.refs
        source = part.at[self.slot(step, lane)] if own else out.at[lane, step]
        target = device(self.x, self.z + 1 - 2 * lane)
        return remote(source, inbox.at[lane, step], send, recv, base + step + 3 * lane, target)

    def slot(self, step, lane):
        return jnp.where(lane == 0, SIDE - 1 - step, step)

    def sends(self, step, lane):
        slot = self.slot(step, lane)
        return ((lane == 0) & (self.z < slot)) | ((lane == 1) & (self.z > slot))

    def fed(self, lane):
        return ((lane == 0) & (self.z > 0)) | ((lane == 1) & (self.z < SIDE - 1))

    def start(self):
        @pl.loop(0, 2 * (SIDE - 1))
        def _(i):
            step, lane = lax.div(i, 2), lax.rem(i, 2)

            @pl.when(self.sends(step, lane) & jnp.logical_not(self.fed(lane)))
            def _():
                self.copy(step, lane, True).start()

    def forward(self):
        part, out, inbox = self.refs[:3]

        @pl.loop(0, 2 * (SIDE - 1))
        def _(i):
            step, lane = lax.div(i, 2), lax.rem(i, 2)

            @pl.when(self.sends(step, lane) & self.fed(lane))
            def _():
                self.copy(step, lane).wait_recv()
                add(out.at[lane, step], part.at[self.slot(step, lane)], inbox.at[lane, step])
                self.copy(step, lane).start()

    def finish(self, total):
        part, out, inbox = self.refs[:3]
        add(total, part.at[self.z])

        @pl.loop(0, 2)
        def _(lane):
            step = jnp.where(lane == 0, SIDE - 1 - self.z, self.z)

            @pl.when(self.fed(lane))
            def _():
                self.copy(step, lane).wait_recv()
                add(total, total, inbox.at[lane, step])

        @pl.loop(0, 2 * (SIDE - 1))
        def _(i):
            step, lane = lax.div(i, 2), lax.rem(i, 2)

            @pl.when(self.sends(step, lane))
            def _():
                self.copy(step, lane).wait_send()


CHAIN_SUM = [
    pltpu.VMEM((2, SIDE - 1, HALF, WIDTH), jnp.bfloat16),
    pltpu.VMEM((2, SIDE - 1, HALF, WIDTH), jnp.bfloat16),
]


def semaphores(count):
    return [pltpu.SemaphoreType.DMA((count,)), pltpu.SemaphoreType.DMA((count,))]


def call(kernel, name, number, out, scratch, flops=0, specs=None):
    def run(*args):
        return pl.pallas_call(
            kernel,
            out_shape=out,
            in_specs=specs or [VMEM] * len(args),
            out_specs=jax.tree.map(lambda _: VMEM, out),
            scratch_shapes=scratch,
            compiler_params=pltpu.CompilerParams(
                collective_id=number,
                has_side_effects=number is not None,
                vmem_limit_bytes=48 * 2**20,
            ),
            cost_estimate=pl.CostEstimate(flops=flops, bytes_accessed=2**25, transcendentals=0),
            name=name,
        )(*args)

    return run


def bf16(*shape):
    return jax.ShapeDtypeStruct(shape, jnp.bfloat16)


def f32(*shape):
    return jax.ShapeDtypeStruct(shape, jnp.float32)


def keep(src, dst, sem):
    copy = pltpu.make_async_copy(src, dst, sem)
    copy.start()
    return copy


def gather_own(image, text, positive, images, texts, places, send, recv, local):
    x, z = place()
    greet(3, True)
    chain = ChainGather(text.at[LO], texts, send, recv, 0)
    ring = RingGather(image, images, send, recv, 6)
    chain.start()
    ring.start()

    def hint(k):
        return remote(positive, places.at[x], send, recv, 11 + k, device(x + k, z))

    @pl.loop(1, SIDE)
    def _(k):
        hint(k).start()

    kept = [
        keep(text.at[LO], texts.at[z], local.at[0]),
        keep(image, images.at[x], local.at[1]),
        keep(positive, places.at[x], local.at[2]),
    ]
    ring.forward()
    chain.forward()
    ring.finish()
    chain.finish()

    @pl.loop(1, SIDE)
    def _(k):
        hint(k).wait()

    for copy in kept:
        copy.wait()


def gather_both(image, text, images, texts, send, recv, local):
    x, z = place()
    greet(2, True)
    chain = ChainGather(text.at[HI], texts, send, recv, 0)
    ring = RingGather(image, images, send, recv, 6)
    chain.start()
    ring.start()
    kept = [
        keep(text.at[HI], texts.at[z], local.at[0]),
        keep(image, images.at[x], local.at[1]),
    ]
    ring.forward()
    chain.forward()
    ring.finish()
    chain.finish()
    for copy in kept:
        copy.wait()


def middle(
    scalars,
    text_lo,
    text_hi,
    own,
    one,
    fetched,
    places,
    back_one,
    part_own,
    part_two,
    part_lo,
    part_hi,
    two,
    part_one,
    total_lo,
    total_hi,
    relay,
    out,
    inbox,
    send,
    recv,
    local,
):
    x, _ = place()
    scale = scalars[0]
    bias = scalars[1]
    greet(2, False)
    ring = RingGather(fetched, two, send, recv, 0)
    ring.start()
    kept = keep(fetched, two.at[x], local.at[0])
    both = ((text_lo, total_lo, 0), (text_hi, total_hi, HALF))
    half = SIDE * HALF

    def products(images, part, marked=None):
        flat = images[...].reshape(TILE, WIDTH)
        back = None
        for texts, total, shift in both:
            whole = texts[...].reshape(half, WIDTH)
            prod = lax.dot_general(
                flat, whole, (((1,), (1,)), ((), ())), preferred_element_type=jnp.float32
            )
            grad = 0.5 * jnp.tanh(0.5 * (scale * prod + bias)) + 0.5
            if marked is not None:
                grad = grad - marked(shift)
            grad = grad.astype(jnp.bfloat16)
            term = jnp.dot(grad, whole, preferred_element_type=jnp.float32)
            back = term if back is None else back + term
            gain = lax.dot_general(
                grad, flat, (((0,), (0,)), ((), ())), preferred_element_type=jnp.float32
            )
            if part is part_one:
                total[...] = gain
            else:
                total[...] += gain
        part[...] = (scale * back).astype(jnp.bfloat16).reshape(SIDE, ROWS, WIDTH)

    def marked(shift):
        lanes = lax.broadcasted_iota(jnp.int32, (ROWS, ROWS), 1)
        diagonal = lax.broadcasted_iota(jnp.int32, (ROWS, ROWS), 0) == lanes
        column = lax.broadcasted_iota(jnp.int32, (ROWS, half), 1)
        chip = lax.div(column, HALF)
        index = x * TILE + chip * ROWS + shift + (column - chip * HALF)
        marks = []
        for slot in range(SIDE):
            spots = jnp.broadcast_to(places[slot].astype(jnp.float32), (ROWS, ROWS))
            spot = jnp.sum(jnp.where(diagonal, spots, 0.0), axis=1, keepdims=True)
            marks.append(jnp.where(index.astype(jnp.float32) == spot, 1.0, 0.0))
        return jnp.concatenate(marks, axis=0)

    products(one, part_one)
    sums = RingSum(part_one, relay, out, inbox, send, recv, 6)
    sums.start()
    ring.forward()
    products(own, part_own, marked)
    sums.forward()
    ring.finish()
    kept.wait()
    products(two, part_two)
    part_lo[...] = total_lo[...].astype(jnp.bfloat16).reshape(SIDE, HALF, WIDTH)
    part_hi[...] = total_hi[...].astype(jnp.bfloat16).reshape(SIDE, HALF, WIDTH)
    sums.finish(back_one)


def sum_both(part, part_text, back, total, relay, out, inbox, chain_out, chain_in, send, recv):
    greet(2, True)
    sums = RingSum(part, relay, out, inbox, send, recv, 0)
    chain = ChainSum(part_text, chain_out, chain_in, send, recv, 6)
    sums.start()
    chain.start()
    sums.forward()
    chain.forward()
    sums.finish(back)
    chain.finish(total)


def exchange(value, mask, beside):
    count = lax.axis_size("blk")

    def branch(m):
        pairs = [(source, source ^ m) for source in range(count)]

        def run(value, *args):
            return lax.ppermute(value, "blk", pairs), beside(*args)

        return run

    branches = [branch(m) for m in range(1, count)]
    return lambda *args: lax.switch(mask - 1, branches, value, *args)


def unit_rows(x):
    xf = x.astype(jnp.float32)
    norm = jnp.sqrt(jnp.sum(xf * xf, axis=-1, keepdims=True) + 1e-06)
    return (xf / norm, norm)


def prepare(image, text, image_hat, text_hat):
    for source, target in ((image, image_hat), (text, text_hat)):
        target[...] = unit_rows(source[...])[0].astype(jnp.bfloat16)


def norm_backward(grad, value):
    unit, norm = unit_rows(value)
    return ((grad - unit * jnp.sum(unit * grad, axis=-1, keepdims=True)) / norm).astype(jnp.bfloat16)


def conclude(scalars, image, text, own, one, two, text_lo, text_hi, grad_image, grad_text):
    grad = own[...] + one[...].astype(jnp.float32) + two[...].astype(jnp.float32)
    grad_image[...] = norm_backward(grad, image[...])
    for part, rows in ((text_lo, LO), (text_hi, HI)):
        grad_text[rows] = norm_backward(scalars[0] * part[...], text[rows])


def shards(image, text, positive, plan, logit_scale, logit_bias):
    masks = plan[:, 0]
    scalars = jnp.concatenate([logit_scale, logit_bias])
    stack = bf16(SIDE, ROWS, WIDTH)
    half = bf16(SIDE, HALF, WIDTH)
    shard = bf16(ROWS, WIDTH)
    local = pltpu.SemaphoreType.DMA((3,))
    spread = jax.ShapeDtypeStruct((SIDE, 1, ROWS), jnp.int32)

    img_hat, txt_hat = call(prepare, "prepare", None, (shard, shard), [])(image, text)
    first = call(gather_own, "gather_own", 0, (stack, half, spread), [*semaphores(15), local])
    fetched_one, (own, text_lo, places) = exchange(img_hat, masks[0], first)(
        img_hat, txt_hat, positive.reshape(1, ROWS)
    )
    second = call(gather_both, "gather_both", 1, (stack, half), [*semaphores(12), local])
    fetched_two, (one, text_hi) = exchange(img_hat, masks[1], second)(fetched_one, txt_hat)
    third = call(
        middle,
        "middle",
        2,
        (shard, stack, stack, half, half),
        [
            pltpu.VMEM((SIDE, ROWS, WIDTH), jnp.bfloat16),
            pltpu.VMEM((SIDE, ROWS, WIDTH), jnp.bfloat16),
            pltpu.VMEM((SIDE * HALF, WIDTH), jnp.float32),
            pltpu.VMEM((SIDE * HALF, WIDTH), jnp.float32),
            *RING_SUM,
            *semaphores(12),
            local,
        ],
        flops=18 * TILE * TILE * WIDTH,
        specs=[SMEM] + [VMEM] * 6,
    )
    back_one, part_own, part_two, part_lo, part_hi = third(
        scalars, text_lo, text_hi, own, one, fetched_two, places
    )
    scratch = [*RING_SUM, *CHAIN_SUM, *semaphores(12)]
    fourth = call(sum_both, "sum_two", 3, (shard, f32(HALF, WIDTH)), scratch)
    returned_one, (back_two, sum_lo) = exchange(back_one, masks[0], fourth)(part_two, part_lo)
    fifth = call(sum_both, "sum_own", 4, (f32(ROWS, WIDTH), f32(HALF, WIDTH)), scratch)
    returned_two, (img_sum, sum_hi) = exchange(back_two, masks[1], fifth)(part_own, part_hi)
    last = call(conclude, "conclude", None, (shard, shard), [], specs=[SMEM] + [VMEM] * 7)
    return last(scalars, image, text, img_sum, returned_one, returned_two, sum_lo, sum_hi)


def solution(mesh):
    placed = (P(("blk", "row"), None), P(("blk", "row"), None), P(("blk", "row")), P(), P(), P())
    return jax.shard_map(
        shards,
        mesh=mesh,
        in_specs=placed,
        out_specs=(P(("blk", "row"), None), P(("blk", "row"), None)),
        check_vma=False,
    )
```

```python
import functools

import jax
import jax.numpy as jnp
from jax import lax
from jax.experimental import pallas as pl
from jax.experimental.pallas import tpu as pltpu
from jax.sharding import PartitionSpec as P

MESH = pl.DeviceIdType.MESH
VMEM = pl.BlockSpec(memory_space=pltpu.VMEM)
SMEM = pl.BlockSpec(memory_space=pltpu.SMEM)
SIDE = 4
ROWS = 96
HALF = 48
TILE = SIDE * ROWS
WIDTH = 1152


def place():
    row = lax.axis_index("row")
    return lax.div(row, SIDE), lax.rem(row, SIDE)


def device(x, z):
    return {"row": lax.rem(x, SIDE) * SIDE + z}


def remote(src, dst, send, recv, index, target):
    return pltpu.make_async_remote_copy(
        src_ref=src,
        dst_ref=dst,
        send_sem=send.at[index],
        recv_sem=recv.at[index],
        device_id=target,
        device_id_type=MESH,
    )


def greet(offsets=(1, 3), chain=False, partner=None):
    x, z = place()
    barrier = pltpu.get_barrier_semaphore()

    def signal(target):
        pl.semaphore_signal(barrier, inc=1, device_id=target, device_id_type=MESH)

    count = len(offsets)
    for offset in offsets:
        signal(device(x + offset, z))
    if partner is not None:
        signal(partner)
        count += 1
    if chain:
        count = count + jnp.where(z < SIDE - 1, 1, 0) + jnp.where(z > 0, 1, 0)

        @pl.when(z < SIDE - 1)
        def _():
            signal(device(x, z + 1))

        @pl.when(z > 0)
        def _():
            signal(device(x, z - 1))

    pl.semaphore_wait(barrier, count)


def partner_of(mask):
    index = lax.axis_index("blk")
    other = index
    for level in range(5):
        if (mask >> level) & 1:
            bit = lax.rem(lax.div(index, 1 << level), 2)
            other = other + (1 - 2 * bit) * (1 << level)
    return {"blk": other}


LO = pl.ds(0, HALF)
HI = pl.ds(HALF, HALF)


def rows_of(lane):
    return pl.ds(pl.multiple_of(lane * HALF, 16), HALF)


class Ring:
    def lanes(self, step):
        @pl.loop(0, 2)
        def _(lane):
            step(lane)

    def ends(self, lane):
        sign = 1 - 2 * lane
        after = lax.rem(self.x + sign + SIDE, SIDE)
        before = lax.rem(self.x - sign + SIDE, SIDE)
        return after, before, device(after, self.z)

    def start(self):
        self.lanes(lambda lane: self.first(lane).start())
        self.lanes(lambda lane: self.second(lane).start())

    def drain(self):
        def step(lane):
            self.second(lane).wait_recv()
            self.onward(lane).wait_recv()
            for copy in (self.first, self.second, self.onward):
                copy(lane).wait_send()

        self.lanes(step)


class RingGather(Ring):
    def __init__(self, src, dst, send, recv, base):
        self.src, self.dst, self.sems = src, dst, (send, recv)
        self.base = base
        self.x, self.z = place()

    def copy(self, source, slot, rows, index, target):
        return remote(source.at[rows], self.dst.at[slot, rows], *self.sems, self.base + index, target)

    def first(self, lane):
        return self.copy(self.src, self.x, rows_of(lane), lane, self.ends(lane)[2])

    def second(self, lane):
        return self.copy(self.src, self.x, rows_of(1 - lane), 2 + lane, self.ends(lane)[2])

    def onward(self, lane):
        _, before, target = self.ends(lane)
        return self.copy(self.dst.at[before], before, rows_of(lane), 4 + lane, target)

    def forward(self):
        def step(lane):
            self.first(lane).wait_recv()
            self.onward(lane).start()

        self.lanes(step)

    def finish(self):
        self.drain()


class ChainGather:
    def __init__(self, src, dst, send, recv, base):
        self.refs = (src, dst, send, recv, base)
        self.x, self.z = place()

    def copy(self, step, lane, own=False):
        src, dst, send, recv, base = self.refs
        sign = 1 - 2 * lane
        slot = self.z - sign * step
        source = src if own else dst.at[slot]
        target = device(self.x, self.z + sign)
        return remote(source, dst.at[slot], send, recv, base + step + 3 * lane, target)

    def sends(self, step, lane):
        edge = self.z + 1 - 2 * lane
        first = self.z - (1 - 2 * lane) * step
        return (first >= 0) & (first < SIDE) & (edge >= 0) & (edge < SIDE) & (step < SIDE - 1)

    def gets(self, step, lane):
        first = self.z - (1 - 2 * lane) * (step + 1)
        return (first >= 0) & (first < SIDE)

    def start(self):
        @pl.loop(0, 2)
        def _(lane):
            @pl.when(self.sends(0, lane))
            def _():
                self.copy(0, lane, True).start()

    def forward(self):
        @pl.loop(0, 2 * (SIDE - 1))
        def _(i):
            step, lane = lax.div(i, 2), lax.rem(i, 2)

            @pl.when(self.gets(step, lane))
            def _():
                self.copy(step, lane).wait_recv()

            @pl.when(self.sends(step + 1, lane))
            def _():
                self.copy(step + 1, lane).start()

    def finish(self):
        @pl.loop(0, 2 * (SIDE - 1))
        def _(i):
            step, lane = lax.div(i, 2), lax.rem(i, 2)

            @pl.when(self.sends(step, lane))
            def _():
                self.copy(step, lane).wait_send()


def add(out, *terms):
    @pl.loop(0, out.shape[0] // 16)
    def _(i):
        rows = pl.ds(pl.multiple_of(i * 16, 16), 16)
        total = terms[0][rows].astype(jnp.float32)
        for term in terms[1:]:
            total = total + term[rows].astype(jnp.float32)
        out[rows] = total.astype(out.dtype)


class RingSum(Ring):
    def __init__(self, part, relay, out, inbox, send, recv, base):
        self.x, self.z = place()
        self.part, self.relay, self.out, self.inbox = part, relay, out, inbox
        self.sems, self.base = (send, recv), base

    def first(self, lane):
        across = lax.rem(self.x + 2, SIDE)
        source = self.part.at[across, rows_of(lane)]
        return remote(source, self.relay.at[lane], *self.sems, self.base + lane, self.ends(lane)[2])

    def second(self, lane):
        after, _, target = self.ends(lane)
        rows = rows_of(1 - lane)
        source, into = self.part.at[after, rows], self.inbox.at[lane, rows]
        return remote(source, into, *self.sems, self.base + 2 + lane, target)

    def onward(self, lane):
        into = self.inbox.at[lane, rows_of(lane)]
        index, target = self.base + 4 + lane, self.ends(lane)[2]
        return remote(self.out.at[lane], into, *self.sems, index, target)

    def forward(self):
        def step(lane):
            self.first(lane).wait_recv()
            after = self.ends(lane)[0]
            add(self.out.at[lane], self.part.at[after, rows_of(lane)], self.relay.at[lane])
            self.onward(lane).start()

        self.lanes(step)

    def finish(self, total):
        self.drain()
        add(total, self.part.at[self.x], self.inbox.at[0], self.inbox.at[1])


RING_SUM = [
    pltpu.VMEM((2, HALF, WIDTH), jnp.bfloat16),
    pltpu.VMEM((2, HALF, WIDTH), jnp.bfloat16),
    pltpu.VMEM((2, ROWS, WIDTH), jnp.bfloat16),
]


class ChainSum:
    def __init__(self, part, out, inbox, send, recv, base):
        self.refs = (part, out, inbox, send, recv, base)
        self.x, self.z = place()

    def copy(self, step, lane, own=False):
        part, out, inbox, send, recv, base = self.refs
        source = part.at[self.slot(step, lane)] if own else out.at[lane, step]
        target = device(self.x, self.z + 1 - 2 * lane)
        return remote(source, inbox.at[lane, step], send, recv, base + step + 3 * lane, target)

    def slot(self, step, lane):
        return jnp.where(lane == 0, SIDE - 1 - step, step)

    def sends(self, step, lane):
        slot = self.slot(step, lane)
        return ((lane == 0) & (self.z < slot)) | ((lane == 1) & (self.z > slot))

    def fed(self, lane):
        return ((lane == 0) & (self.z > 0)) | ((lane == 1) & (self.z < SIDE - 1))

    def start(self):
        @pl.loop(0, 2 * (SIDE - 1))
        def _(i):
            step, lane = lax.div(i, 2), lax.rem(i, 2)

            @pl.when(self.sends(step, lane) & jnp.logical_not(self.fed(lane)))
            def _():
                self.copy(step, lane, True).start()

    def forward(self):
        part, out, inbox = self.refs[:3]

        @pl.loop(0, 2 * (SIDE - 1))
        def _(i):
            step, lane = lax.div(i, 2), lax.rem(i, 2)

            @pl.when(self.sends(step, lane) & self.fed(lane))
            def _():
                self.copy(step, lane).wait_recv()
                add(out.at[lane, step], part.at[self.slot(step, lane)], inbox.at[lane, step])
                self.copy(step, lane).start()

    def finish(self, total):
        part, out, inbox = self.refs[:3]
        add(total, part.at[self.z])

        @pl.loop(0, 2)
        def _(lane):
            step = jnp.where(lane == 0, SIDE - 1 - self.z, self.z)

            @pl.when(self.fed(lane))
            def _():
                self.copy(step, lane).wait_recv()
                add(total, total, inbox.at[lane, step])

        @pl.loop(0, 2 * (SIDE - 1))
        def _(i):
            step, lane = lax.div(i, 2), lax.rem(i, 2)

            @pl.when(self.sends(step, lane))
            def _():
                self.copy(step, lane).wait_send()


CHAIN_SUM = [
    pltpu.VMEM((2, SIDE - 1, HALF, WIDTH), jnp.bfloat16),
    pltpu.VMEM((2, SIDE - 1, HALF, WIDTH), jnp.bfloat16),
]


def semaphores(count):
    return [pltpu.SemaphoreType.DMA((count,)), pltpu.SemaphoreType.DMA((count,))]


def call(kernel, name, number, out, scratch, flops=0, specs=None):
    def run(*args):
        return pl.pallas_call(
            kernel,
            out_shape=out,
            in_specs=specs or [VMEM] * len(args),
            out_specs=jax.tree.map(lambda _: VMEM, out),
            scratch_shapes=scratch,
            compiler_params=pltpu.CompilerParams(
                collective_id=number,
                has_side_effects=number is not None,
                vmem_limit_bytes=48 * 2**20,
            ),
            cost_estimate=pl.CostEstimate(flops=flops, bytes_accessed=2**25, transcendentals=0),
            name=name,
        )(*args)

    return run


def bf16(*shape):
    return jax.ShapeDtypeStruct(shape, jnp.bfloat16)


def f32(*shape):
    return jax.ShapeDtypeStruct(shape, jnp.float32)


def keep(src, dst, sem):
    copy = pltpu.make_async_copy(src, dst, sem)
    copy.start()
    return copy


def swap(source, target, send, recv, index, partner):
    copy = remote(source, target, send, recv, index, partner)
    copy.start()
    return copy


def gather(mask, image, text, mine, images, texts, fetched, send, recv, local):
    x, z = place()
    partner = partner_of(mask)
    greet(chain=True, partner=partner)
    fetch = swap(mine, fetched, send, recv, 12, partner)
    chain = ChainGather(text, texts, send, recv, 0)
    ring = RingGather(image, images, send, recv, 6)
    chain.start()
    ring.start()
    kept = [keep(text, texts.at[z], local.at[0]), keep(image, images.at[x], local.at[1])]
    ring.forward()
    chain.forward()
    ring.finish()
    chain.finish()
    for copy in kept:
        copy.wait()
    fetch.wait()


def middle(
    scalars,
    text_lo,
    text_hi,
    own,
    one,
    fetched,
    positive,
    back_one,
    part_own,
    part_two,
    part_lo,
    part_hi,
    two,
    part_one,
    grad_lo,
    grad_hi,
    total_lo,
    total_hi,
    places,
    relay,
    out,
    inbox,
    send,
    recv,
    local,
):
    x, z = place()
    scale = scalars[0]
    bias = scalars[1]
    greet((1, 2, 3))
    ring = RingGather(fetched, two, send, recv, 0)
    ring.start()
    kept = [keep(fetched, two.at[x], local.at[0]), keep(positive, places.at[x], local.at[1])]

    def hint(k):
        return remote(positive, places.at[x], send, recv, 11 + k, device(x + k, z))

    @pl.loop(1, SIDE)
    def _(k):
        hint(k).start()

    both = ((text_lo, grad_lo, total_lo, 0), (text_hi, grad_hi, total_hi, HALF))
    half = SIDE * HALF

    def products(images, part, marked=None):
        flat = images[...].reshape(TILE, WIDTH)
        for texts, grads, _, shift in both:
            whole = texts[...].reshape(half, WIDTH)
            prod = lax.dot_general(
                flat, whole, (((1,), (1,)), ((), ())), preferred_element_type=jnp.float32
            )
            grad = 0.5 * jnp.tanh(0.5 * (scale * prod + bias)) + 0.5
            if marked is not None:
                grad = grad - marked(shift)
            grads[...] = grad.astype(jnp.bfloat16)

        @pl.loop(0, WIDTH // TILE)
        def _(tile):
            columns = pl.ds(pl.multiple_of(tile * TILE, 128), TILE)
            left = images[:, :, columns].reshape(TILE, TILE)
            back = 0.0
            for texts, grads, total, _ in both:
                right = texts[:, :, columns].reshape(half, TILE)
                back = back + jnp.dot(grads[...], right, preferred_element_type=jnp.float32)
                gain = lax.dot_general(
                    grads[...], left, (((0,), (0,)), ((), ())), preferred_element_type=jnp.float32
                )
                total[:, columns] = gain if part is part_one else total[:, columns] + gain
            back = (scale * back).astype(jnp.bfloat16)
            part[:, :, columns] = back.reshape(SIDE, ROWS, TILE)

    def marked(shift):
        lanes = lax.broadcasted_iota(jnp.int32, (ROWS, ROWS), 1)
        diagonal = lax.broadcasted_iota(jnp.int32, (ROWS, ROWS), 0) == lanes
        column = lax.broadcasted_iota(jnp.int32, (ROWS, half), 1)
        chip = lax.div(column, HALF)
        index = x * TILE + chip * ROWS + shift + (column - chip * HALF)
        marks = []
        for slot in range(SIDE):
            spots = jnp.broadcast_to(places[slot].astype(jnp.float32), (ROWS, ROWS))
            spot = jnp.sum(jnp.where(diagonal, spots, 0.0), axis=1, keepdims=True)
            marks.append(jnp.where(index.astype(jnp.float32) == spot, 1.0, 0.0))
        return jnp.concatenate(marks, axis=0)

    products(one, part_one)

    @pl.loop(1, SIDE)
    def _(k):
        hint(k).wait()

    kept[1].wait()
    sums = RingSum(part_one, relay, out, inbox, send, recv, 6)
    sums.start()
    ring.forward()
    products(own, part_own, marked)
    sums.forward()
    ring.finish()
    kept[0].wait()
    products(two, part_two)

    @pl.loop(0, SIDE)
    def _(slot):
        rows = pl.ds(pl.multiple_of(slot * HALF, 16), HALF)
        add(part_lo.at[slot], total_lo.at[rows])
        add(part_hi.at[slot], total_hi.at[rows])

    sums.finish(back_one)


def sum_both(mask, part, part_text, mine, ring_total, chain_total, returned, *scratch):
    relay, out, inbox, chain_out, chain_in, send, recv = scratch
    partner = partner_of(mask)
    greet(chain=True, partner=partner)
    giving = swap(mine, returned, send, recv, 12, partner)
    chain = ChainSum(part_text, chain_out, chain_in, send, recv, 6)
    sums = RingSum(part, relay, out, inbox, send, recv, 0)
    chain.start()
    sums.start()
    sums.forward()
    chain.forward()
    sums.finish(ring_total)
    chain.finish(chain_total)
    giving.wait()


def for_mask(mask, kernel, name, first, out, scratch):
    count = lax.axis_size("blk")
    branches = [
        call(functools.partial(kernel, m), name, first + m, out, scratch) for m in range(1, count)
    ]
    return lambda *args: lax.switch(mask - 1, branches, *args)


def unit_rows(x):
    xf = x.astype(jnp.float32)
    norm = jnp.sqrt(jnp.sum(xf * xf, axis=-1, keepdims=True) + 1e-06)
    return (xf / norm, norm)


def prepare(image, text, image_hat, text_lo, text_hi):
    image_hat[...] = unit_rows(image[...])[0].astype(jnp.bfloat16)
    for rows, target in ((LO, text_lo), (HI, text_hi)):
        target[...] = unit_rows(text[rows])[0].astype(jnp.bfloat16)


def norm_backward(grad, value):
    unit, norm = unit_rows(value)
    return ((grad - unit * jnp.sum(unit * grad, axis=-1, keepdims=True)) / norm).astype(jnp.bfloat16)


def conclude(scalars, image, text, own, one, two, text_lo, text_hi, grad_image, grad_text):
    grad = own[...].astype(jnp.float32) + one[...].astype(jnp.float32) + two[...].astype(jnp.float32)
    grad_image[...] = norm_backward(grad, image[...])
    for part, rows in ((text_lo, LO), (text_hi, HI)):
        grad_text[rows] = norm_backward(scalars[0] * part[...], text[rows])


def shards(image, text, positive, plan, logit_scale, logit_bias):
    masks = plan[:, 0]
    scalars = jnp.concatenate([logit_scale, logit_bias])
    stack = bf16(SIDE, ROWS, WIDTH)
    half = bf16(SIDE, HALF, WIDTH)
    shard = bf16(ROWS, WIDTH)
    local = pltpu.SemaphoreType.DMA((2,))

    ready = call(prepare, "prepare", None, (shard, bf16(HALF, WIDTH), bf16(HALF, WIDTH)), [])
    img_hat, txt_lo, txt_hi = ready(image, text)
    shapes, scratch = (stack, half, shard), [*semaphores(13), local]
    first = for_mask(masks[0], gather, "gather", 0, shapes, scratch)
    own, text_lo, fetched_one = first(img_hat, txt_lo, img_hat)
    second = for_mask(masks[1], gather, "gather", 0, shapes, scratch)
    one, text_hi, fetched_two = second(fetched_one, txt_hi, img_hat)
    third = call(
        middle,
        "middle",
        0,
        (shard, stack, stack, half, half),
        [
            pltpu.VMEM((SIDE, ROWS, WIDTH), jnp.bfloat16),
            pltpu.VMEM((SIDE, ROWS, WIDTH), jnp.bfloat16),
            pltpu.VMEM((TILE, SIDE * HALF), jnp.bfloat16),
            pltpu.VMEM((TILE, SIDE * HALF), jnp.bfloat16),
            pltpu.VMEM((SIDE * HALF, WIDTH), jnp.float32),
            pltpu.VMEM((SIDE * HALF, WIDTH), jnp.float32),
            pltpu.VMEM((SIDE, 1, ROWS), jnp.int32),
            *RING_SUM,
            *semaphores(15),
            local,
        ],
        flops=18 * TILE * TILE * WIDTH,
        specs=[SMEM] + [VMEM] * 6,
    )
    back_one, part_own, part_two, part_lo, part_hi = third(
        scalars, text_lo, text_hi, own, one, fetched_two, positive.reshape(1, ROWS)
    )
    shapes, scratch = (shard, f32(HALF, WIDTH), shard), [*RING_SUM, *CHAIN_SUM, *semaphores(13)]
    fourth = for_mask(masks[0], sum_both, "sum_both", 31, shapes, scratch)
    back_two, sum_lo, returned_one = fourth(part_two, part_lo, back_one)
    fifth = for_mask(masks[1], sum_both, "sum_both", 31, shapes, scratch)
    img_sum, sum_hi, returned_two = fifth(part_own, part_hi, back_two)
    last = call(conclude, "conclude", None, (shard, shard), [], specs=[SMEM] + [VMEM] * 7)
    return last(scalars, image, text, img_sum, returned_one, returned_two, sum_lo, sum_hi)


def solution(mesh):
    placed = (P(("blk", "row"), None), P(("blk", "row"), None), P(("blk", "row")), P(), P(), P())
    return jax.shard_map(
        shards,
        mesh=mesh,
        in_specs=placed,
        out_specs=(P(("blk", "row"), None), P(("blk", "row"), None)),
        check_vma=False,
    )
```

```python
import jax
import jax.numpy as jnp
from jax import lax
from jax.experimental import pallas as pl
from jax.experimental.pallas import tpu as pltpu
from jax.sharding import PartitionSpec as P

MESH = pl.DeviceIdType.MESH
VMEM = pl.BlockSpec(memory_space=pltpu.VMEM)
SMEM = pl.BlockSpec(memory_space=pltpu.SMEM)
SIDE = 4
ROWS = 96
HALF = 48
TILE = SIDE * ROWS
WIDTH = 1152


def place():
    row = lax.axis_index("row")
    return lax.div(row, SIDE), lax.rem(row, SIDE)


def device(x, z):
    return {"row": lax.rem(x, SIDE) * SIDE + z}


def remote(src, dst, send, recv, index, target):
    return pltpu.make_async_remote_copy(
        src_ref=src,
        dst_ref=dst,
        send_sem=send.at[index],
        recv_sem=recv.at[index],
        device_id=target,
        device_id_type=MESH,
    )


def greet(offsets):
    x, z = place()
    barrier = pltpu.get_barrier_semaphore()

    def signal(target):
        pl.semaphore_signal(barrier, inc=1, device_id=target, device_id_type=MESH)

    for offset in offsets:
        signal(device(x + offset, z))

    @pl.when(z < SIDE - 1)
    def _():
        signal(device(x, z + 1))

    @pl.when(z > 0)
    def _():
        signal(device(x, z - 1))

    ends = jnp.where(z < SIDE - 1, 1, 0) + jnp.where(z > 0, 1, 0)
    pl.semaphore_wait(barrier, len(offsets) + ends)


def rows_of(lane):
    return pl.ds(pl.multiple_of(lane * HALF, 16), HALF)


class Ring:
    def lanes(self, step):
        @pl.loop(0, 2)
        def _(lane):
            step(lane)

    def ends(self, lane):
        sign = 1 - 2 * lane
        after = lax.rem(self.x + sign + SIDE, SIDE)
        before = lax.rem(self.x - sign + SIDE, SIDE)
        return after, before, device(after, self.z)

    def start(self):
        self.lanes(lambda lane: self.first(lane).start())
        self.lanes(lambda lane: self.second(lane).start())

    def drain(self):
        def step(lane):
            self.second(lane).wait_recv()
            self.onward(lane).wait_recv()
            for copy in (self.first, self.second, self.onward):
                copy(lane).wait_send()

        self.lanes(step)


class RingGather(Ring):
    def __init__(self, src, dst, send, recv, base):
        self.src, self.dst, self.sems = src, dst, (send, recv)
        self.base = base
        self.x, self.z = place()

    def copy(self, source, slot, rows, index, target):
        return remote(source.at[rows], self.dst.at[slot, rows], *self.sems, self.base + index, target)

    def first(self, lane):
        return self.copy(self.src, self.x, rows_of(lane), lane, self.ends(lane)[2])

    def second(self, lane):
        return self.copy(self.src, self.x, rows_of(1 - lane), 2 + lane, self.ends(lane)[2])

    def onward(self, lane):
        _, before, target = self.ends(lane)
        return self.copy(self.dst.at[before], before, rows_of(lane), 4 + lane, target)

    def forward(self):
        def step(lane):
            self.first(lane).wait_recv()
            self.onward(lane).start()

        self.lanes(step)

    def finish(self):
        self.drain()


class ChainGather:
    def __init__(self, src, dst, send, recv, base):
        self.refs = (src, dst, send, recv, base)
        self.x, self.z = place()

    def copy(self, step, lane, own=False):
        src, dst, send, recv, base = self.refs
        sign = 1 - 2 * lane
        slot = self.z - sign * step
        source = src if own else dst.at[slot]
        target = device(self.x, self.z + sign)
        return remote(source, dst.at[slot], send, recv, base + step + 3 * lane, target)

    def sends(self, step, lane):
        edge = self.z + 1 - 2 * lane
        first = self.z - (1 - 2 * lane) * step
        return (first >= 0) & (first < SIDE) & (edge >= 0) & (edge < SIDE) & (step < SIDE - 1)

    def gets(self, step, lane):
        first = self.z - (1 - 2 * lane) * (step + 1)
        return (first >= 0) & (first < SIDE)

    def start(self):
        @pl.loop(0, 2)
        def _(lane):
            @pl.when(self.sends(0, lane))
            def _():
                self.copy(0, lane, True).start()

    def forward(self, step):
        @pl.loop(0, 2)
        def _(lane):
            @pl.when(self.gets(step, lane))
            def _():
                self.copy(step, lane).wait_recv()

            @pl.when(self.sends(step + 1, lane))
            def _():
                self.copy(step + 1, lane).start()

    def finish(self):
        @pl.loop(0, 2 * (SIDE - 1))
        def _(i):
            step, lane = lax.div(i, 2), lax.rem(i, 2)

            @pl.when(self.sends(step, lane))
            def _():
                self.copy(step, lane).wait_send()


def add(out, *terms):
    @pl.loop(0, out.shape[0] // 16)
    def _(i):
        rows = pl.ds(pl.multiple_of(i * 16, 16), 16)
        total = terms[0][rows].astype(jnp.float32)
        for term in terms[1:]:
            total = total + term[rows].astype(jnp.float32)
        out[rows] = total.astype(out.dtype)


class RingSum(Ring):
    def __init__(self, part, relay, out, inbox, send, recv, base):
        self.x, self.z = place()
        self.part, self.relay, self.out, self.inbox = part, relay, out, inbox
        self.sems, self.base = (send, recv), base

    def first(self, lane):
        across = lax.rem(self.x + 2, SIDE)
        source = self.part.at[across, rows_of(lane)]
        return remote(source, self.relay.at[lane], *self.sems, self.base + lane, self.ends(lane)[2])

    def second(self, lane):
        after, _, target = self.ends(lane)
        rows = rows_of(1 - lane)
        source, into = self.part.at[after, rows], self.inbox.at[lane, rows]
        return remote(source, into, *self.sems, self.base + 2 + lane, target)

    def onward(self, lane):
        into = self.inbox.at[lane, rows_of(lane)]
        index, target = self.base + 4 + lane, self.ends(lane)[2]
        return remote(self.out.at[lane], into, *self.sems, index, target)

    def forward(self):
        def step(lane):
            self.first(lane).wait_recv()
            after = self.ends(lane)[0]
            add(self.out.at[lane], self.part.at[after, rows_of(lane)], self.relay.at[lane])
            self.onward(lane).start()

        self.lanes(step)

    def finish(self, total):
        self.drain()
        add(total, self.part.at[self.x], self.inbox.at[0], self.inbox.at[1])


RING_SUM = [
    pltpu.VMEM((3, 2, HALF, WIDTH), jnp.bfloat16),
    pltpu.VMEM((3, 2, HALF, WIDTH), jnp.bfloat16),
    pltpu.VMEM((3, 2, ROWS, WIDTH), jnp.bfloat16),
]


class ChainSum:
    def __init__(self, part, out, inbox, send, recv, base):
        self.refs = (part, out, inbox, send, recv, base)
        self.x, self.z = place()

    def copy(self, step, lane, own=False):
        part, out, inbox, send, recv, base = self.refs
        source = part.at[self.slot(step, lane)] if own else out.at[lane, step]
        target = device(self.x, self.z + 1 - 2 * lane)
        return remote(source, inbox.at[lane, step], send, recv, base + step + 3 * lane, target)

    def slot(self, step, lane):
        return jnp.where(lane == 0, SIDE - 1 - step, step)

    def sends(self, step, lane):
        slot = self.slot(step, lane)
        return ((lane == 0) & (self.z < slot)) | ((lane == 1) & (self.z > slot))

    def fed(self, lane):
        return ((lane == 0) & (self.z > 0)) | ((lane == 1) & (self.z < SIDE - 1))

    def start(self):
        @pl.loop(0, 2 * (SIDE - 1))
        def _(i):
            step, lane = lax.div(i, 2), lax.rem(i, 2)

            @pl.when(self.sends(step, lane) & jnp.logical_not(self.fed(lane)))
            def _():
                self.copy(step, lane, True).start()

    def forward(self, step):
        part, out, inbox = self.refs[:3]

        @pl.loop(0, 2)
        def _(i):
            lane = lax.rem(i + lax.div(self.z, 2), 2)

            @pl.when(self.sends(step, lane) & self.fed(lane))
            def _():
                self.copy(step, lane).wait_recv()
                add(out.at[lane, step], part.at[self.slot(step, lane)], inbox.at[lane, step])
                self.copy(step, lane).start()

    def finish(self, total):
        part, out, inbox = self.refs[:3]
        add(total, part.at[self.z])

        @pl.loop(0, 2)
        def _(lane):
            step = jnp.where(lane == 0, SIDE - 1 - self.z, self.z)

            @pl.when(self.fed(lane))
            def _():
                self.copy(step, lane).wait_recv()
                add(total, total, inbox.at[lane, step])

        @pl.loop(0, 2 * (SIDE - 1))
        def _(i):
            step, lane = lax.div(i, 2), lax.rem(i, 2)

            @pl.when(self.sends(step, lane))
            def _():
                self.copy(step, lane).wait_send()


CHAIN_SUM = [
    pltpu.VMEM((2, SIDE - 1, ROWS, WIDTH), jnp.bfloat16),
    pltpu.VMEM((2, SIDE - 1, ROWS, WIDTH), jnp.bfloat16),
]


def semaphores(count):
    return [pltpu.SemaphoreType.DMA((count,)), pltpu.SemaphoreType.DMA((count,))]


def call(kernel, name, number, out, scratch, flops=0, specs=None):
    def run(*args):
        return pl.pallas_call(
            kernel,
            out_shape=out,
            in_specs=specs or [VMEM] * len(args),
            out_specs=jax.tree.map(lambda _: VMEM, out),
            scratch_shapes=scratch,
            compiler_params=pltpu.CompilerParams(
                collective_id=number,
                has_side_effects=number is not None,
                vmem_limit_bytes=48 * 2**20,
            ),
            cost_estimate=pl.CostEstimate(flops=flops, bytes_accessed=2**25, transcendentals=0),
            name=name,
        )(*args)

    return run


def bf16(*shape):
    return jax.ShapeDtypeStruct(shape, jnp.bfloat16)


def f32(*shape):
    return jax.ShapeDtypeStruct(shape, jnp.float32)


def keep(src, dst, sem):
    copy = pltpu.make_async_copy(src, dst, sem)
    copy.start()
    return copy


def core(scalars, text, image, one, two, positive, back_one, back_two, own_sum, text_sum, *scratch):
    texts, piles, parts, part_text, total, places = scratch[:6]
    relays, outs, inboxes, chain_out, chain_in, send, recv, local = scratch[6:]
    x, z = place()
    scale = scalars[0]
    bias = scalars[1]
    greet((1, 2, 3))
    chain = ChainGather(text, texts, send, recv, 0)
    sources = (image, one, two)
    rings = [RingGather(sources[k], piles.at[k], send, recv, 6 * k + 6) for k in range(3)]

    def hint(k):
        return remote(positive, places.at[x], send, recv, 23 + k, device(x + k, z))

    rings[0].start()
    chain.start()

    @pl.loop(1, SIDE)
    def _(k):
        hint(k).start()

    kept = [keep(text, texts.at[z], local.at[0]), keep(positive, places.at[x], local.at[1])]
    kept += [keep(sources[k], piles.at[k, x], local.at[2 + k]) for k in range(3)]
    rings[0].forward()
    rings[1].start()
    chain.forward(0)
    rings[1].forward()
    rings[2].start()
    chain.forward(1)
    rings[2].forward()
    chain.forward(2)
    chain.finish()
    for copy in kept:
        copy.wait()

    @pl.loop(1, SIDE)
    def _(k):
        hint(k).wait()

    def products(k):
        flat = piles[k].reshape(TILE, WIDTH)
        whole = texts[...].reshape(TILE, WIDTH)
        prod = lax.dot_general(
            flat, whole, (((1,), (1,)), ((), ())), preferred_element_type=jnp.float32
        )
        grad = 0.5 * jnp.tanh(0.5 * (scale * prod + bias)) + 0.5
        if k == 0:
            grad = grad - marked()
        grad = grad.astype(jnp.bfloat16)
        back = scale * jnp.dot(grad, whole, preferred_element_type=jnp.float32)
        parts[k] = back.astype(jnp.bfloat16).reshape(SIDE, ROWS, WIDTH)
        return grad, flat

    def gains(k, grad, flat):
        gain = lax.dot_general(
            grad, flat, (((0,), (0,)), ((), ())), preferred_element_type=jnp.float32
        )
        if k == 0:
            total[...] = gain
        elif k == 1:
            total[...] += gain
        else:
            gain = total[...] + gain
            part_text[...] = gain.astype(jnp.bfloat16).reshape(SIDE, ROWS, WIDTH)

    def marked():
        lanes = lax.broadcasted_iota(jnp.int32, (ROWS, ROWS), 1)
        diagonal = lax.broadcasted_iota(jnp.int32, (ROWS, ROWS), 0) == lanes
        index = (lax.broadcasted_iota(jnp.int32, (ROWS, TILE), 1) + x * TILE).astype(jnp.float32)
        marks = []
        for slot in range(SIDE):
            spots = jnp.broadcast_to(places[slot].astype(jnp.float32), (ROWS, ROWS))
            spot = jnp.sum(jnp.where(diagonal, spots, 0.0), axis=1, keepdims=True)
            marks.append(jnp.where(index == spot, 1.0, 0.0))
        return jnp.concatenate(marks, axis=0)

    sums = [
        RingSum(parts.at[k], relays.at[k], outs.at[k], inboxes.at[k], send, recv, 6 * k + 33)
        for k in range(3)
    ]
    chain = ChainSum(part_text, chain_out, chain_in, send, recv, 27)
    rings[0].finish()
    gain = products(0)
    sums[0].start()
    gains(0, *gain)
    rings[1].finish()
    gain = products(1)
    sums[1].start()
    gains(1, *gain)
    sums[0].forward()
    rings[2].finish()
    gain = products(2)
    sums[2].start()
    gains(2, *gain)
    chain.start()
    sums[1].forward()
    chain.forward(0)
    sums[2].forward()
    chain.forward(1)
    chain.forward(2)
    for ring, result in zip(sums, (own_sum, back_one, back_two)):
        ring.finish(result)
    chain.finish(text_sum)


def exchange(value, mask):
    count = lax.axis_size("blk")

    def branch(m):
        pairs = [(source, source ^ m) for source in range(count)]
        return lambda v: lax.ppermute(v, "blk", pairs)

    return lax.switch(mask - 1, [branch(m) for m in range(1, count)], value)


def unit_rows(x):
    xf = x.astype(jnp.float32)
    norm = jnp.sqrt(jnp.sum(xf * xf, axis=-1, keepdims=True) + 1e-06)
    return (xf / norm, norm)


def prepare(image, text, image_hat, text_hat):
    for source, target in ((image, image_hat), (text, text_hat)):
        target[...] = unit_rows(source[...])[0].astype(jnp.bfloat16)


def norm_backward(grad, value):
    unit, norm = unit_rows(value)
    return ((grad - unit * jnp.sum(unit * grad, axis=-1, keepdims=True)) / norm).astype(jnp.bfloat16)


def conclude(scalars, image, text, own, one, two, txt, grad_image, grad_text):
    grad = own[...].astype(jnp.float32) + one[...].astype(jnp.float32) + two[...].astype(jnp.float32)
    grad_image[...] = norm_backward(grad, image[...])
    grad_text[...] = norm_backward(scalars[0] * txt[...], text[...])


def shards(image, text, positive, plan, logit_scale, logit_bias):
    masks = plan[:, 0]
    scalars = jnp.concatenate([logit_scale, logit_bias])
    shard = bf16(ROWS, WIDTH)
    wide = f32(ROWS, WIDTH)

    img_hat, txt_hat = call(prepare, "prepare", None, (shard, shard), [])(image, text)
    fetched = [exchange(img_hat, masks[step]) for step in range(2)]
    middle = call(
        core,
        "core",
        0,
        (shard, shard, wide, wide),
        [
            pltpu.VMEM((SIDE, ROWS, WIDTH), jnp.bfloat16),
            pltpu.VMEM((3, SIDE, ROWS, WIDTH), jnp.bfloat16),
            pltpu.VMEM((3, SIDE, ROWS, WIDTH), jnp.bfloat16),
            pltpu.VMEM((SIDE, ROWS, WIDTH), jnp.bfloat16),
            pltpu.VMEM((TILE, WIDTH), jnp.float32),
            pltpu.VMEM((SIDE, 1, ROWS), jnp.int32),
            *RING_SUM,
            *CHAIN_SUM,
            *semaphores(51),
            pltpu.SemaphoreType.DMA((5,)),
        ],
        flops=18 * TILE * TILE * WIDTH,
        specs=[SMEM] + [VMEM] * 5,
    )
    back_one, back_two, own_sum, text_sum = middle(
        scalars, txt_hat, img_hat, *fetched, positive.reshape(1, ROWS)
    )
    returned = [exchange(back, masks[step]) for step, back in enumerate((back_one, back_two))]
    last = call(conclude, "conclude", None, (shard, shard), [], specs=[SMEM] + [VMEM] * 6)
    return last(scalars, image, text, own_sum, *returned, text_sum)


def solution(mesh):
    placed = (P(("blk", "row"), None), P(("blk", "row"), None), P(("blk", "row")), P(), P(), P())
    return jax.shard_map(
        shards,
        mesh=mesh,
        in_specs=placed,
        out_specs=(P(("blk", "row"), None), P(("blk", "row"), None)),
        check_vma=False,
    )
```

```python
import jax
import jax.numpy as jnp
from jax import lax
from jax.experimental import pallas as pl
from jax.experimental.pallas import tpu as pltpu
from jax.sharding import PartitionSpec as P

MESH = pl.DeviceIdType.MESH
VMEM = pl.BlockSpec(memory_space=pltpu.VMEM)
SMEM = pl.BlockSpec(memory_space=pltpu.SMEM)
SIDE = 4
ROWS = 96
HALF = 48
TILE = SIDE * ROWS
WIDTH = 1152


def place():
    row = lax.axis_index("row")
    return lax.div(row, SIDE), lax.rem(row, SIDE)


def device(x, z):
    return {"row": lax.rem(x, SIDE) * SIDE + z}


def remote(src, dst, send, recv, index, target):
    return pltpu.make_async_remote_copy(
        src_ref=src,
        dst_ref=dst,
        send_sem=send.at[index],
        recv_sem=recv.at[index],
        device_id=target,
        device_id_type=MESH,
    )


def greet(offsets):
    x, z = place()
    barrier = pltpu.get_barrier_semaphore()

    def signal(target):
        pl.semaphore_signal(barrier, inc=1, device_id=target, device_id_type=MESH)

    for offset in offsets:
        signal(device(x + offset, z))

    @pl.when(z < SIDE - 1)
    def _():
        signal(device(x, z + 1))

    @pl.when(z > 0)
    def _():
        signal(device(x, z - 1))

    ends = jnp.where(z < SIDE - 1, 1, 0) + jnp.where(z > 0, 1, 0)
    pl.semaphore_wait(barrier, len(offsets) + ends)


def rows_of(lane):
    return pl.ds(pl.multiple_of(lane * HALF, 16), HALF)


class Ring:
    def lanes(self, step):
        @pl.loop(0, 2)
        def _(lane):
            step(lane)

    def ends(self, lane):
        sign = 1 - 2 * lane
        after = lax.rem(self.x + sign + SIDE, SIDE)
        before = lax.rem(self.x - sign + SIDE, SIDE)
        return after, before, device(after, self.z)

    def start(self):
        self.lanes(lambda lane: self.first(lane).start())
        self.lanes(lambda lane: self.second(lane).start())

    def drain(self):
        def step(lane):
            self.second(lane).wait_recv()
            self.onward(lane).wait_recv()
            for copy in (self.first, self.second, self.onward):
                copy(lane).wait_send()

        self.lanes(step)


class RingGather(Ring):
    def __init__(self, src, dst, send, recv, base):
        self.src, self.dst, self.sems = src, dst, (send, recv)
        self.base = base
        self.x, self.z = place()

    def copy(self, source, slot, rows, index, target):
        return remote(source.at[rows], self.dst.at[slot, rows], *self.sems, self.base + index, target)

    def first(self, lane):
        return self.copy(self.src, self.x, rows_of(lane), lane, self.ends(lane)[2])

    def second(self, lane):
        return self.copy(self.src, self.x, rows_of(1 - lane), 2 + lane, self.ends(lane)[2])

    def onward(self, lane):
        _, before, target = self.ends(lane)
        return self.copy(self.dst.at[before], before, rows_of(lane), 4 + lane, target)

    def forward(self):
        def step(lane):
            self.first(lane).wait_recv()
            self.onward(lane).start()

        self.lanes(step)

    def finish(self):
        self.drain()


class ChainGather:
    def __init__(self, src, dst, send, recv, base):
        self.refs = (src, dst, send, recv, base)
        self.x, self.z = place()

    def copy(self, step, lane, own=False):
        src, dst, send, recv, base = self.refs
        sign = 1 - 2 * lane
        slot = self.z - sign * step
        source = src if own else dst.at[slot]
        target = device(self.x, self.z + sign)
        return remote(source, dst.at[slot], send, recv, base + step + 3 * lane, target)

    def sends(self, step, lane):
        edge = self.z + 1 - 2 * lane
        first = self.z - (1 - 2 * lane) * step
        return (first >= 0) & (first < SIDE) & (edge >= 0) & (edge < SIDE) & (step < SIDE - 1)

    def gets(self, step, lane):
        first = self.z - (1 - 2 * lane) * (step + 1)
        return (first >= 0) & (first < SIDE)

    def start(self):
        @pl.loop(0, 2)
        def _(lane):
            @pl.when(self.sends(0, lane))
            def _():
                self.copy(0, lane, True).start()

    def forward(self, step):
        @pl.loop(0, 2)
        def _(lane):
            @pl.when(self.gets(step, lane))
            def _():
                self.copy(step, lane).wait_recv()

            @pl.when(self.sends(step + 1, lane))
            def _():
                self.copy(step + 1, lane).start()

    def finish(self):
        @pl.loop(0, 2 * (SIDE - 1))
        def _(i):
            step, lane = lax.div(i, 2), lax.rem(i, 2)

            @pl.when(self.sends(step, lane))
            def _():
                self.copy(step, lane).wait_send()


def add(out, *terms):
    @pl.loop(0, out.shape[0] // 16)
    def _(i):
        rows = pl.ds(pl.multiple_of(i * 16, 16), 16)
        total = terms[0][rows].astype(jnp.float32)
        for term in terms[1:]:
            total = total + term[rows].astype(jnp.float32)
        out[rows] = total.astype(out.dtype)


class RingSum(Ring):
    def __init__(self, part, relay, out, inbox, send, recv, base):
        self.x, self.z = place()
        self.part, self.relay, self.out, self.inbox = part, relay, out, inbox
        self.sems, self.base = (send, recv), base

    def first(self, lane):
        across = lax.rem(self.x + 2, SIDE)
        source = self.part.at[across, rows_of(lane)]
        return remote(source, self.relay.at[lane], *self.sems, self.base + lane, self.ends(lane)[2])

    def second(self, lane):
        after, _, target = self.ends(lane)
        rows = rows_of(1 - lane)
        source, into = self.part.at[after, rows], self.inbox.at[lane, rows]
        return remote(source, into, *self.sems, self.base + 2 + lane, target)

    def onward(self, lane):
        into = self.inbox.at[lane, rows_of(lane)]
        index, target = self.base + 4 + lane, self.ends(lane)[2]
        return remote(self.out.at[lane], into, *self.sems, index, target)

    def forward(self):
        def step(lane):
            self.first(lane).wait_recv()
            after = self.ends(lane)[0]
            add(self.out.at[lane], self.part.at[after, rows_of(lane)], self.relay.at[lane])
            self.onward(lane).start()

        self.lanes(step)

    def finish(self, total):
        self.drain()
        add(total, self.part.at[self.x], self.inbox.at[0], self.inbox.at[1])


RING_SUM = [
    pltpu.VMEM((2, HALF, WIDTH), jnp.bfloat16),
    pltpu.VMEM((2, HALF, WIDTH), jnp.bfloat16),
    pltpu.VMEM((2, ROWS, WIDTH), jnp.bfloat16),
]


class ChainSum:
    def __init__(self, part, out, inbox, send, recv, base):
        self.refs = (part, out, inbox, send, recv, base)
        self.x, self.z = place()

    def copy(self, step, lane, own=False):
        part, out, inbox, send, recv, base = self.refs
        source = part.at[self.slot(step, lane)] if own else out.at[lane, step]
        target = device(self.x, self.z + 1 - 2 * lane)
        return remote(source, inbox.at[lane, step], send, recv, base + step + 3 * lane, target)

    def slot(self, step, lane):
        return jnp.where(lane == 0, SIDE - 1 - step, step)

    def sends(self, step, lane):
        slot = self.slot(step, lane)
        return ((lane == 0) & (self.z < slot)) | ((lane == 1) & (self.z > slot))

    def fed(self, lane):
        return ((lane == 0) & (self.z > 0)) | ((lane == 1) & (self.z < SIDE - 1))

    def start(self):
        @pl.loop(0, 2 * (SIDE - 1))
        def _(i):
            step, lane = lax.div(i, 2), lax.rem(i, 2)

            @pl.when(self.sends(step, lane) & jnp.logical_not(self.fed(lane)))
            def _():
                self.copy(step, lane, True).start()

    def forward(self, step):
        part, out, inbox = self.refs[:3]

        @pl.loop(0, 2)
        def _(i):
            lane = lax.rem(i + lax.div(self.z, 2), 2)

            @pl.when(self.sends(step, lane) & self.fed(lane))
            def _():
                self.copy(step, lane).wait_recv()
                add(out.at[lane, step], part.at[self.slot(step, lane)], inbox.at[lane, step])
                self.copy(step, lane).start()

    def finish(self, total):
        part, out, inbox = self.refs[:3]
        add(total, part.at[self.z])

        @pl.loop(0, 2)
        def _(lane):
            step = jnp.where(lane == 0, SIDE - 1 - self.z, self.z)

            @pl.when(self.fed(lane))
            def _():
                self.copy(step, lane).wait_recv()
                add(total, total, inbox.at[lane, step])

        @pl.loop(0, 2 * (SIDE - 1))
        def _(i):
            step, lane = lax.div(i, 2), lax.rem(i, 2)

            @pl.when(self.sends(step, lane))
            def _():
                self.copy(step, lane).wait_send()


CHAIN_SUM = [
    pltpu.VMEM((2, SIDE - 1, ROWS, WIDTH), jnp.bfloat16),
    pltpu.VMEM((2, SIDE - 1, ROWS, WIDTH), jnp.bfloat16),
]


def semaphores(count):
    return [pltpu.SemaphoreType.DMA((count,)), pltpu.SemaphoreType.DMA((count,))]


def call(kernel, name, number, out, scratch, flops=0, specs=None):
    def run(*args):
        return pl.pallas_call(
            kernel,
            out_shape=out,
            in_specs=specs or [VMEM] * len(args),
            out_specs=jax.tree.map(lambda _: VMEM, out),
            scratch_shapes=scratch,
            compiler_params=pltpu.CompilerParams(
                collective_id=number,
                has_side_effects=number is not None,
                vmem_limit_bytes=48 * 2**20,
            ),
            cost_estimate=pl.CostEstimate(flops=flops, bytes_accessed=2**25, transcendentals=0),
            name=name,
        )(*args)

    return run


def bf16(*shape):
    return jax.ShapeDtypeStruct(shape, jnp.bfloat16)


def f32(*shape):
    return jax.ShapeDtypeStruct(shape, jnp.float32)


def keep(src, dst, sem):
    copy = pltpu.make_async_copy(src, dst, sem)
    copy.start()
    return copy


def gather(pair, images, texts, send, recv, local):
    x, z = place()
    greet((1, 3))
    chain = ChainGather(pair.at[1], texts, send, recv, 0)
    ring = RingGather(pair.at[0], images, send, recv, 6)
    chain.start()
    ring.start()
    kept = [keep(pair.at[0], images.at[x], local.at[0]), keep(pair.at[1], texts.at[z], local.at[1])]
    ring.forward()
    for step in range(SIDE - 1):
        chain.forward(step)
    ring.finish()
    chain.finish()
    for copy in kept:
        copy.wait()


def core(
    scalars,
    own_images,
    own_texts,
    one_images,
    one_texts,
    pair,
    positive,
    image_sum,
    text_sum,
    *scratch,
):
    two_images, two_texts, part_image, part_text, ga, gt, places = scratch[:7]
    relay, out, inbox, chain_out, chain_in, send, recv, local = scratch[7:]
    x, z = place()
    scale = scalars[0]
    bias = scalars[1]
    greet((1, 2, 3))
    chain = ChainGather(pair.at[1], two_texts, send, recv, 0)
    ring = RingGather(pair.at[0], two_images, send, recv, 6)

    def hint(k):
        return remote(positive, places.at[x], send, recv, 11 + k, device(x + k, z))

    @pl.loop(1, SIDE)
    def _(k):
        hint(k).start()

    ring.start()
    chain.start()
    kept = [
        keep(positive, places.at[x], local.at[0]),
        keep(pair.at[0], two_images.at[x], local.at[1]),
        keep(pair.at[1], two_texts.at[z], local.at[2]),
    ]

    def weights(images, texts):
        prod = lax.dot_general(
            images[...].reshape(TILE, WIDTH),
            texts[...].reshape(TILE, WIDTH),
            (((1,), (1,)), ((), ())),
            preferred_element_type=jnp.float32,
        )
        return 0.5 * jnp.tanh(0.5 * (scale * prod + bias)) + 0.5

    def image_term(grad, texts):
        right = texts[...].reshape(TILE, WIDTH)
        return jnp.dot(grad, right, preferred_element_type=jnp.float32)

    def text_term(grad, images):
        right = images[...].reshape(TILE, WIDTH)
        return lax.dot_general(
            grad, right, (((0,), (0,)), ((), ())), preferred_element_type=jnp.float32
        )

    def marked():
        lanes = lax.broadcasted_iota(jnp.int32, (ROWS, ROWS), 1)
        diagonal = lax.broadcasted_iota(jnp.int32, (ROWS, ROWS), 0) == lanes
        index = (lax.broadcasted_iota(jnp.int32, (ROWS, TILE), 1) + x * TILE).astype(jnp.float32)
        marks = []
        for slot in range(SIDE):
            spots = jnp.broadcast_to(places[slot].astype(jnp.float32), (ROWS, ROWS))
            spot = jnp.sum(jnp.where(diagonal, spots, 0.0), axis=1, keepdims=True)
            marks.append(jnp.where(index == spot, 1.0, 0.0))
        return jnp.concatenate(marks, axis=0)

    grad = weights(one_images, own_texts).astype(jnp.bfloat16)
    gt[...] = text_term(grad, one_images)
    ring.forward()
    grad = weights(own_images, one_texts).astype(jnp.bfloat16)
    ga[...] = image_term(grad, one_texts)
    chain.forward(0)

    @pl.loop(1, SIDE)
    def _(k):
        hint(k).wait()

    for copy in kept:
        copy.wait()
    grad = (weights(own_images, own_texts) - marked()).astype(jnp.bfloat16)
    gt[...] += text_term(grad, own_images)
    ga[...] += image_term(grad, own_texts)
    ring.finish()
    grad = weights(two_images, own_texts).astype(jnp.bfloat16)
    total = gt[...] + text_term(grad, two_images)
    part_text[...] = total.astype(jnp.bfloat16).reshape(SIDE, ROWS, WIDTH)
    chain.forward(1)
    sums = ChainSum(part_text, chain_out, chain_in, send, recv, 15)
    sums.start()
    chain.forward(2)
    chain.finish()
    grad = weights(own_images, two_texts).astype(jnp.bfloat16)
    total = scale * (ga[...] + image_term(grad, two_texts))
    part_image[...] = total.astype(jnp.bfloat16).reshape(SIDE, ROWS, WIDTH)
    ring = RingSum(part_image, relay, out, inbox, send, recv, 21)
    ring.start()
    sums.forward(0)
    ring.forward()
    sums.forward(1)
    sums.forward(2)
    ring.finish(image_sum)
    sums.finish(text_sum)


def exchange(value, mask, beside):
    count = lax.axis_size("blk")

    def branch(m):
        pairs = [(source, source ^ m) for source in range(count)]
        return lambda v, w: (lax.ppermute(v, "blk", pairs), beside(w))

    branches = [branch(m) for m in range(1, count)]
    return lambda other: lax.switch(mask - 1, branches, value, other)


def unit_rows(x):
    xf = x.astype(jnp.float32)
    norm = jnp.sqrt(jnp.sum(xf * xf, axis=-1, keepdims=True) + 1e-06)
    return (xf / norm, norm)


def prepare(image, text, pair):
    for slot, source in enumerate((image, text)):
        pair[slot] = unit_rows(source[...])[0].astype(jnp.bfloat16)


def norm_backward(grad, value):
    unit, norm = unit_rows(value)
    return ((grad - unit * jnp.sum(unit * grad, axis=-1, keepdims=True)) / norm).astype(jnp.bfloat16)


def conclude(scalars, image, text, image_sum, text_sum, grad_image, grad_text):
    grad_image[...] = norm_backward(image_sum[...], image[...])
    grad_text[...] = norm_backward(scalars[0] * text_sum[...], text[...])


def shards(image, text, positive, plan, logit_scale, logit_bias):
    masks = plan[:, 0]
    scalars = jnp.concatenate([logit_scale, logit_bias])
    shard = bf16(ROWS, WIDTH)
    wide = f32(ROWS, WIDTH)
    stack = bf16(SIDE, ROWS, WIDTH)
    room = pltpu.VMEM((SIDE, ROWS, WIDTH), jnp.bfloat16)
    total = pltpu.VMEM((TILE, WIDTH), jnp.float32)

    own = call(prepare, "prepare", None, bf16(2, ROWS, WIDTH), [])(image, text)
    scratch = [*semaphores(12), pltpu.SemaphoreType.DMA((2,))]
    beside = call(gather, "gather", 0, (stack, stack), scratch)
    one, (own_images, own_texts) = exchange(own, masks[0], beside)(own)
    two, (one_images, one_texts) = exchange(own, masks[1], beside)(one)
    middle = call(
        core,
        "core",
        1,
        (wide, wide),
        [
            *[room] * 4,
            *[total] * 2,
            pltpu.VMEM((SIDE, 1, ROWS), jnp.int32),
            *RING_SUM,
            *CHAIN_SUM,
            *semaphores(27),
            pltpu.SemaphoreType.DMA((3,)),
        ],
        flops=24 * TILE * TILE * WIDTH,
        specs=[SMEM] + [VMEM] * 6,
    )
    image_sum, text_sum = middle(
        scalars, own_images, own_texts, one_images, one_texts, two, positive.reshape(1, ROWS)
    )
    last = call(conclude, "conclude", None, (shard, shard), [], specs=[SMEM] + [VMEM] * 4)
    return last(scalars, image, text, image_sum, text_sum)


def solution(mesh):
    placed = (P(("blk", "row"), None), P(("blk", "row"), None), P(("blk", "row")), P(), P(), P())
    return jax.shard_map(
        shards,
        mesh=mesh,
        in_specs=placed,
        out_specs=(P(("blk", "row"), None), P(("blk", "row"), None)),
        check_vma=False,
    )
```

```python
import jax
import jax.numpy as jnp
from jax import lax
from jax.experimental import pallas as pl
from jax.experimental.pallas import tpu as pltpu
from jax.sharding import PartitionSpec as P

MESH = pl.DeviceIdType.MESH
VMEM = pl.BlockSpec(memory_space=pltpu.VMEM)
SMEM = pl.BlockSpec(memory_space=pltpu.SMEM)
SIDE = 4
ROWS = 96
HALF = 48
TILE = SIDE * ROWS
WIDTH = 1152


def place():
    row = lax.axis_index("row")
    return lax.div(row, SIDE), lax.rem(row, SIDE)


def device(x, z):
    return {"row": lax.rem(x, SIDE) * SIDE + z}


def remote(src, dst, send, recv, index, target):
    return pltpu.make_async_remote_copy(
        src_ref=src,
        dst_ref=dst,
        send_sem=send.at[index],
        recv_sem=recv.at[index],
        device_id=target,
        device_id_type=MESH,
    )


def greet(offsets):
    x, z = place()
    barrier = pltpu.get_barrier_semaphore()

    def signal(target):
        pl.semaphore_signal(barrier, inc=1, device_id=target, device_id_type=MESH)

    for offset in offsets:
        signal(device(x + offset, z))

    @pl.when(z < SIDE - 1)
    def _():
        signal(device(x, z + 1))

    @pl.when(z > 0)
    def _():
        signal(device(x, z - 1))

    ends = jnp.where(z < SIDE - 1, 1, 0) + jnp.where(z > 0, 1, 0)
    pl.semaphore_wait(barrier, len(offsets) + ends)


HALVES = (pl.ds(0, HALF), pl.ds(HALF, HALF))


def rows_of(lane):
    return pl.ds(pl.multiple_of(lane * HALF, 16), HALF)


class Ring:
    def lanes(self, step):
        @pl.loop(0, 2)
        def _(lane):
            step(lane)

    def ends(self, lane):
        sign = 1 - 2 * lane
        after = lax.rem(self.x + sign + SIDE, SIDE)
        before = lax.rem(self.x - sign + SIDE, SIDE)
        return after, before, device(after, self.z)

    def start(self):
        self.lanes(lambda lane: self.first(lane).start())
        self.lanes(lambda lane: self.second(lane).start())

    def drain(self):
        def step(lane):
            self.second(lane).wait_recv()
            self.onward(lane).wait_recv()
            for copy in (self.first, self.second, self.onward):
                copy(lane).wait_send()

        self.lanes(step)


class RingGather(Ring):
    def __init__(self, src, dst, send, recv, base):
        self.src, self.dst, self.sems = src, dst, (send, recv)
        self.base = base
        self.x, self.z = place()

    def copy(self, source, slot, rows, index, target):
        return remote(source.at[rows], self.dst.at[slot, rows], *self.sems, self.base + index, target)

    def first(self, lane):
        return self.copy(self.src, self.x, rows_of(lane), lane, self.ends(lane)[2])

    def second(self, lane):
        return self.copy(self.src, self.x, rows_of(1 - lane), 2 + lane, self.ends(lane)[2])

    def onward(self, lane):
        _, before, target = self.ends(lane)
        return self.copy(self.dst.at[before], before, rows_of(lane), 4 + lane, target)

    def forward(self):
        def step(lane):
            self.first(lane).wait_recv()
            self.onward(lane).start()

        self.lanes(step)

    def finish(self):
        self.drain()


class ChainGather:
    def __init__(self, src, dst, send, recv, base):
        self.refs = (src, dst, send, recv, base)
        self.x, self.z = place()

    def copy(self, step, lane, own=False):
        src, dst, send, recv, base = self.refs
        sign = 1 - 2 * lane
        slot = self.z - sign * step
        source = src if own else dst.at[slot]
        target = device(self.x, self.z + sign)
        return remote(source, dst.at[slot], send, recv, base + step + 3 * lane, target)

    def sends(self, step, lane):
        edge = self.z + 1 - 2 * lane
        first = self.z - (1 - 2 * lane) * step
        return (first >= 0) & (first < SIDE) & (edge >= 0) & (edge < SIDE) & (step < SIDE - 1)

    def gets(self, step, lane):
        first = self.z - (1 - 2 * lane) * (step + 1)
        return (first >= 0) & (first < SIDE)

    def start(self):
        @pl.loop(0, 2)
        def _(lane):
            @pl.when(self.sends(0, lane))
            def _():
                self.copy(0, lane, True).start()

    def forward(self, step):
        @pl.loop(0, 2)
        def _(lane):
            @pl.when(self.gets(step, lane))
            def _():
                self.copy(step, lane).wait_recv()

            @pl.when(self.sends(step + 1, lane))
            def _():
                self.copy(step + 1, lane).start()

    def finish(self):
        @pl.loop(0, 2 * (SIDE - 1))
        def _(i):
            step, lane = lax.div(i, 2), lax.rem(i, 2)

            @pl.when(self.sends(step, lane))
            def _():
                self.copy(step, lane).wait_send()


def add(out, *terms):
    @pl.loop(0, out.shape[0] // 16)
    def _(i):
        rows = pl.ds(pl.multiple_of(i * 16, 16), 16)
        total = terms[0][rows].astype(jnp.float32)
        for term in terms[1:]:
            total = total + term[rows].astype(jnp.float32)
        out[rows] = total.astype(out.dtype)


class RingSum(Ring):
    def __init__(self, part, relay, out, inbox, send, recv, base):
        self.x, self.z = place()
        self.part, self.relay, self.out, self.inbox = part, relay, out, inbox
        self.sems, self.base = (send, recv), base

    def first(self, lane):
        across = lax.rem(self.x + 2, SIDE)
        source = self.part.at[across, rows_of(lane)]
        return remote(source, self.relay.at[lane], *self.sems, self.base + lane, self.ends(lane)[2])

    def second(self, lane):
        after, _, target = self.ends(lane)
        rows = rows_of(1 - lane)
        source, into = self.part.at[after, rows], self.inbox.at[lane, rows]
        return remote(source, into, *self.sems, self.base + 2 + lane, target)

    def onward(self, lane):
        into = self.inbox.at[lane, rows_of(lane)]
        index, target = self.base + 4 + lane, self.ends(lane)[2]
        return remote(self.out.at[lane], into, *self.sems, index, target)

    def forward(self):
        def step(lane):
            self.first(lane).wait_recv()
            after = self.ends(lane)[0]
            add(self.out.at[lane], self.part.at[after, rows_of(lane)], self.relay.at[lane])
            self.onward(lane).start()

        self.lanes(step)

    def finish(self, total):
        self.drain()
        add(total, self.part.at[self.x], self.inbox.at[0], self.inbox.at[1])


RING_SUM = [
    pltpu.VMEM((2, HALF, WIDTH), jnp.bfloat16),
    pltpu.VMEM((2, HALF, WIDTH), jnp.bfloat16),
    pltpu.VMEM((2, ROWS, WIDTH), jnp.bfloat16),
]


class ChainSum:
    def __init__(self, part, out, inbox, send, recv, base):
        self.refs = (part, out, inbox, send, recv, base)
        self.x, self.z = place()

    def copy(self, step, lane, own=False):
        part, out, inbox, send, recv, base = self.refs
        source = part.at[self.slot(step, lane)] if own else out.at[lane, step]
        target = device(self.x, self.z + 1 - 2 * lane)
        return remote(source, inbox.at[lane, step], send, recv, base + step + 3 * lane, target)

    def slot(self, step, lane):
        return jnp.where(lane == 0, SIDE - 1 - step, step)

    def sends(self, step, lane):
        slot = self.slot(step, lane)
        return ((lane == 0) & (self.z < slot)) | ((lane == 1) & (self.z > slot))

    def fed(self, lane):
        return ((lane == 0) & (self.z > 0)) | ((lane == 1) & (self.z < SIDE - 1))

    def start(self):
        @pl.loop(0, 2 * (SIDE - 1))
        def _(i):
            step, lane = lax.div(i, 2), lax.rem(i, 2)

            @pl.when(self.sends(step, lane) & jnp.logical_not(self.fed(lane)))
            def _():
                self.copy(step, lane, True).start()

    def forward(self, step):
        part, out, inbox = self.refs[:3]

        @pl.loop(0, 2)
        def _(i):
            lane = lax.rem(i + lax.div(self.z, 2), 2)

            @pl.when(self.sends(step, lane) & self.fed(lane))
            def _():
                self.copy(step, lane).wait_recv()
                add(out.at[lane, step], part.at[self.slot(step, lane)], inbox.at[lane, step])
                self.copy(step, lane).start()

    def finish(self, total):
        part, out, inbox = self.refs[:3]
        add(total, part.at[self.z])

        @pl.loop(0, 2)
        def _(lane):
            step = jnp.where(lane == 0, SIDE - 1 - self.z, self.z)

            @pl.when(self.fed(lane))
            def _():
                self.copy(step, lane).wait_recv()
                add(total, total, inbox.at[lane, step])

        @pl.loop(0, 2 * (SIDE - 1))
        def _(i):
            step, lane = lax.div(i, 2), lax.rem(i, 2)

            @pl.when(self.sends(step, lane))
            def _():
                self.copy(step, lane).wait_send()


CHAIN_SUM = [
    pltpu.VMEM((2, 2, SIDE - 1, HALF, WIDTH), jnp.bfloat16),
    pltpu.VMEM((2, 2, SIDE - 1, HALF, WIDTH), jnp.bfloat16),
]


def semaphores(count):
    return [pltpu.SemaphoreType.DMA((count,)), pltpu.SemaphoreType.DMA((count,))]


def call(kernel, name, number, out, scratch, flops=0, specs=None):
    def run(*args):
        return pl.pallas_call(
            kernel,
            out_shape=out,
            in_specs=specs or [VMEM] * len(args),
            out_specs=jax.tree.map(lambda _: VMEM, out),
            scratch_shapes=scratch,
            compiler_params=pltpu.CompilerParams(
                collective_id=number,
                has_side_effects=number is not None,
                vmem_limit_bytes=48 * 2**20,
            ),
            cost_estimate=pl.CostEstimate(flops=flops, bytes_accessed=2**25, transcendentals=0),
            name=name,
        )(*args)

    return run


def bf16(*shape):
    return jax.ShapeDtypeStruct(shape, jnp.bfloat16)


def f32(*shape):
    return jax.ShapeDtypeStruct(shape, jnp.float32)


def keep(src, dst, sem):
    copy = pltpu.make_async_copy(src, dst, sem)
    copy.start()
    return copy


def chain_gathers(src, dst, send, recv, base):
    return [
        ChainGather(src.at[rows], dst.at[:, rows], send, recv, base + 6 * part)
        for part, rows in enumerate(HALVES)
    ]


def gather(pair, images, texts, send, recv, local):
    x, z = place()
    greet((1, 3))
    chains = chain_gathers(pair.at[1], texts, send, recv, 6)
    ring = RingGather(pair.at[0], images, send, recv, 0)
    for chain in chains:
        chain.start()
    ring.start()
    kept = [keep(pair.at[0], images.at[x], local.at[0]), keep(pair.at[1], texts.at[z], local.at[1])]
    ring.forward()
    for step in range(SIDE - 1):
        for chain in chains:
            chain.forward(step)
    ring.finish()
    for chain in chains:
        chain.finish()
    for copy in kept:
        copy.wait()


def core(
    scalars,
    own_images,
    own_texts,
    one_images,
    one_texts,
    pair,
    positive,
    image_sum,
    text_sum,
    *scratch,
):
    two_images, two_texts, part_image, part_text, ga, gt, places = scratch[:7]
    relay, out, inbox, chain_out, chain_in, send, recv, local = scratch[7:]
    x, z = place()
    scale = scalars[0]
    bias = scalars[1]
    greet((1, 2, 3))
    chains = chain_gathers(pair.at[1], two_texts, send, recv, 0)
    ring = RingGather(pair.at[0], two_images, send, recv, 12)

    def hint(k):
        return remote(positive, places.at[x], send, recv, 17 + k, device(x + k, z))

    @pl.loop(1, SIDE)
    def _(k):
        hint(k).start()

    ring.start()
    for chain in chains:
        chain.start()
    kept = [
        keep(positive, places.at[x], local.at[0]),
        keep(pair.at[0], two_images.at[x], local.at[1]),
        keep(pair.at[1], two_texts.at[z], local.at[2]),
    ]

    def weights(images, texts):
        prod = lax.dot_general(
            images[...].reshape(TILE, WIDTH),
            texts[...].reshape(TILE, WIDTH),
            (((1,), (1,)), ((), ())),
            preferred_element_type=jnp.float32,
        )
        return 0.5 * jnp.tanh(0.5 * (scale * prod + bias)) + 0.5

    def image_term(grad, texts):
        right = texts[...].reshape(TILE, WIDTH)
        return jnp.dot(grad, right, preferred_element_type=jnp.float32)

    def text_term(grad, images):
        right = images[...].reshape(TILE, WIDTH)
        return lax.dot_general(
            grad, right, (((0,), (0,)), ((), ())), preferred_element_type=jnp.float32
        )

    def marked():
        lanes = lax.broadcasted_iota(jnp.int32, (ROWS, ROWS), 1)
        diagonal = lax.broadcasted_iota(jnp.int32, (ROWS, ROWS), 0) == lanes
        index = (lax.broadcasted_iota(jnp.int32, (ROWS, TILE), 1) + x * TILE).astype(jnp.float32)
        marks = []
        for slot in range(SIDE):
            spots = jnp.broadcast_to(places[slot].astype(jnp.float32), (ROWS, ROWS))
            spot = jnp.sum(jnp.where(diagonal, spots, 0.0), axis=1, keepdims=True)
            marks.append(jnp.where(index == spot, 1.0, 0.0))
        return jnp.concatenate(marks, axis=0)

    grad = weights(one_images, own_texts).astype(jnp.bfloat16)
    gt[...] = text_term(grad, one_images)
    ring.forward()
    grad = weights(own_images, one_texts).astype(jnp.bfloat16)
    ga[...] = image_term(grad, one_texts)
    for chain in chains:
        chain.forward(0)

    @pl.loop(1, SIDE)
    def _(k):
        hint(k).wait()

    for copy in kept:
        copy.wait()
    grad = (weights(own_images, own_texts) - marked()).astype(jnp.bfloat16)
    gt[...] += text_term(grad, own_images)
    ga[...] += image_term(grad, own_texts)
    ring.finish()
    grad = weights(two_images, own_texts).astype(jnp.bfloat16)
    total = gt[...] + text_term(grad, two_images)
    part_text[...] = total.astype(jnp.bfloat16).reshape(SIDE, ROWS, WIDTH)
    for chain in chains:
        chain.forward(1)
    sums = [
        ChainSum(part_text.at[:, rows], chain_out.at[k], chain_in.at[k], send, recv, 21 + 6 * k)
        for k, rows in enumerate(HALVES)
    ]
    for total in sums:
        total.start()
    for chain in chains:
        chain.forward(2)
        chain.finish()
    grad = weights(own_images, two_texts).astype(jnp.bfloat16)
    total = scale * (ga[...] + image_term(grad, two_texts))
    part_image[...] = total.astype(jnp.bfloat16).reshape(SIDE, ROWS, WIDTH)
    ring = RingSum(part_image, relay, out, inbox, send, recv, 33)
    ring.start()
    for total in sums:
        total.forward(0)
    ring.forward()
    for step in (1, 2):
        for total in sums:
            total.forward(step)
    ring.finish(image_sum)
    for total, rows in zip(sums, HALVES):
        total.finish(text_sum.at[rows])


def exchange(value, mask, beside):
    count = lax.axis_size("blk")

    def branch(m):
        pairs = [(source, source ^ m) for source in range(count)]
        return lambda v, w: (lax.ppermute(v, "blk", pairs), beside(w))

    branches = [branch(m) for m in range(1, count)]
    return lambda other: lax.switch(mask - 1, branches, value, other)


def unit_rows(x):
    xf = x.astype(jnp.float32)
    norm = jnp.sqrt(jnp.sum(xf * xf, axis=-1, keepdims=True) + 1e-06)
    return (xf / norm, norm)


def prepare(image, text, pair):
    for slot, source in enumerate((image, text)):
        pair[slot] = unit_rows(source[...])[0].astype(jnp.bfloat16)


def norm_backward(grad, value):
    unit, norm = unit_rows(value)
    return ((grad - unit * jnp.sum(unit * grad, axis=-1, keepdims=True)) / norm).astype(jnp.bfloat16)


def conclude(scalars, image, text, image_sum, text_sum, grad_image, grad_text):
    grad_image[...] = norm_backward(image_sum[...], image[...])
    grad_text[...] = norm_backward(scalars[0] * text_sum[...], text[...])


def shards(image, text, positive, plan, logit_scale, logit_bias):
    masks = plan[:, 0]
    scalars = jnp.concatenate([logit_scale, logit_bias])
    shard = bf16(ROWS, WIDTH)
    wide = f32(ROWS, WIDTH)
    stack = bf16(SIDE, ROWS, WIDTH)
    room = pltpu.VMEM((SIDE, ROWS, WIDTH), jnp.bfloat16)
    total = pltpu.VMEM((TILE, WIDTH), jnp.float32)

    own = call(prepare, "prepare", None, bf16(2, ROWS, WIDTH), [])(image, text)
    scratch = [*semaphores(18), pltpu.SemaphoreType.DMA((2,))]
    beside = call(gather, "gather", 0, (stack, stack), scratch)
    one, (own_images, own_texts) = exchange(own, masks[0], beside)(own)
    two, (one_images, one_texts) = exchange(own, masks[1], beside)(one)
    middle = call(
        core,
        "core",
        1,
        (wide, wide),
        [
            *[room] * 4,
            *[total] * 2,
            pltpu.VMEM((SIDE, 1, ROWS), jnp.int32),
            *RING_SUM,
            *CHAIN_SUM,
            *semaphores(39),
            pltpu.SemaphoreType.DMA((3,)),
        ],
        flops=24 * TILE * TILE * WIDTH,
        specs=[SMEM] + [VMEM] * 6,
    )
    image_sum, text_sum = middle(
        scalars, own_images, own_texts, one_images, one_texts, two, positive.reshape(1, ROWS)
    )
    last = call(conclude, "conclude", None, (shard, shard), [], specs=[SMEM] + [VMEM] * 4)
    return last(scalars, image, text, image_sum, text_sum)


def solution(mesh):
    placed = (P(("blk", "row"), None), P(("blk", "row"), None), P(("blk", "row")), P(), P(), P())
    return jax.shard_map(
        shards,
        mesh=mesh,
        in_specs=placed,
        out_specs=(P(("blk", "row"), None), P(("blk", "row"), None)),
        check_vma=False,
    )
```

```python
import jax
import jax.numpy as jnp
from jax import lax
from jax.experimental import pallas as pl
from jax.experimental.pallas import tpu as pltpu
from jax.sharding import PartitionSpec as P

MESH = pl.DeviceIdType.MESH
VMEM = pl.BlockSpec(memory_space=pltpu.VMEM)
SMEM = pl.BlockSpec(memory_space=pltpu.SMEM)
SIDE = 4
ROWS = 96
HALF = 48
TILE = SIDE * ROWS
WIDTH = 1152


def place():
    row = lax.axis_index("row")
    return lax.div(row, SIDE), lax.rem(row, SIDE)


def device(x, z):
    return {"row": lax.rem(x, SIDE) * SIDE + z}


def remote(src, dst, send, recv, index, target):
    return pltpu.make_async_remote_copy(
        src_ref=src,
        dst_ref=dst,
        send_sem=send.at[index],
        recv_sem=recv.at[index],
        device_id=target,
        device_id_type=MESH,
    )


def greet(offsets):
    x, z = place()
    barrier = pltpu.get_barrier_semaphore()

    def signal(target):
        pl.semaphore_signal(barrier, inc=1, device_id=target, device_id_type=MESH)

    for offset in offsets:
        signal(device(x + offset, z))

    @pl.when(z < SIDE - 1)
    def _():
        signal(device(x, z + 1))

    @pl.when(z > 0)
    def _():
        signal(device(x, z - 1))

    ends = jnp.where(z < SIDE - 1, 1, 0) + jnp.where(z > 0, 1, 0)
    pl.semaphore_wait(barrier, len(offsets) + ends)


HALVES = (pl.ds(0, HALF), pl.ds(HALF, HALF))


def rows_of(lane):
    return pl.ds(pl.multiple_of(lane * HALF, 16), HALF)


class Ring:
    def lanes(self, step):
        @pl.loop(0, 2)
        def _(lane):
            step(lane)

    def ends(self, lane):
        sign = 1 - 2 * lane
        after = lax.rem(self.x + sign + SIDE, SIDE)
        before = lax.rem(self.x - sign + SIDE, SIDE)
        return after, before, device(after, self.z)

    def start(self):
        self.lanes(lambda lane: self.first(lane).start())
        self.lanes(lambda lane: self.second(lane).start())

    def drain(self):
        def step(lane):
            self.second(lane).wait_recv()
            self.onward(lane).wait_recv()
            for copy in (self.first, self.second, self.onward):
                copy(lane).wait_send()

        self.lanes(step)


class RingGather(Ring):
    def __init__(self, src, dst, send, recv, base):
        self.src, self.dst, self.sems = src, dst, (send, recv)
        self.base = base
        self.x, self.z = place()

    def copy(self, source, slot, rows, index, target):
        return remote(source.at[rows], self.dst.at[slot, rows], *self.sems, self.base + index, target)

    def first(self, lane):
        return self.copy(self.src, self.x, rows_of(lane), lane, self.ends(lane)[2])

    def second(self, lane):
        return self.copy(self.src, self.x, rows_of(1 - lane), 2 + lane, self.ends(lane)[2])

    def onward(self, lane):
        _, before, target = self.ends(lane)
        return self.copy(self.dst.at[before], before, rows_of(lane), 4 + lane, target)

    def forward(self):
        def step(lane):
            self.first(lane).wait_recv()
            self.onward(lane).start()

        self.lanes(step)

    def finish(self):
        self.drain()


class ChainGather:
    def __init__(self, src, dst, send, recv, base):
        self.refs = (src, dst, send, recv, base)
        self.x, self.z = place()

    def copy(self, step, lane, own=False):
        src, dst, send, recv, base = self.refs
        sign = 1 - 2 * lane
        slot = self.z - sign * step
        source = src if own else dst.at[slot]
        target = device(self.x, self.z + sign)
        return remote(source, dst.at[slot], send, recv, base + step + 3 * lane, target)

    def sends(self, step, lane):
        edge = self.z + 1 - 2 * lane
        first = self.z - (1 - 2 * lane) * step
        return (first >= 0) & (first < SIDE) & (edge >= 0) & (edge < SIDE) & (step < SIDE - 1)

    def gets(self, step, lane):
        first = self.z - (1 - 2 * lane) * (step + 1)
        return (first >= 0) & (first < SIDE)

    def start(self):
        @pl.loop(0, 2)
        def _(lane):
            @pl.when(self.sends(0, lane))
            def _():
                self.copy(0, lane, True).start()

    def forward(self, step):
        @pl.loop(0, 2)
        def _(lane):
            @pl.when(self.gets(step, lane))
            def _():
                self.copy(step, lane).wait_recv()

            @pl.when(self.sends(step + 1, lane))
            def _():
                self.copy(step + 1, lane).start()

    def finish(self):
        @pl.loop(0, 2 * (SIDE - 1))
        def _(i):
            step, lane = lax.div(i, 2), lax.rem(i, 2)

            @pl.when(self.sends(step, lane))
            def _():
                self.copy(step, lane).wait_send()


def add(out, *terms):
    @pl.loop(0, out.shape[0] // 16)
    def _(i):
        rows = pl.ds(pl.multiple_of(i * 16, 16), 16)
        total = terms[0][rows].astype(jnp.float32)
        for term in terms[1:]:
            total = total + term[rows].astype(jnp.float32)
        out[rows] = total.astype(out.dtype)


class RingSum(Ring):
    def __init__(self, part, relay, out, inbox, send, recv, base):
        self.x, self.z = place()
        self.part, self.relay, self.out, self.inbox = part, relay, out, inbox
        self.sems, self.base = (send, recv), base

    def first(self, lane):
        across = lax.rem(self.x + 2, SIDE)
        source = self.part.at[across, rows_of(lane)]
        return remote(source, self.relay.at[lane], *self.sems, self.base + lane, self.ends(lane)[2])

    def second(self, lane):
        after, _, target = self.ends(lane)
        rows = rows_of(1 - lane)
        source, into = self.part.at[after, rows], self.inbox.at[lane, rows]
        return remote(source, into, *self.sems, self.base + 2 + lane, target)

    def onward(self, lane):
        into = self.inbox.at[lane, rows_of(lane)]
        index, target = self.base + 4 + lane, self.ends(lane)[2]
        return remote(self.out.at[lane], into, *self.sems, index, target)

    def forward(self):
        def step(lane):
            self.first(lane).wait_recv()
            after = self.ends(lane)[0]
            add(self.out.at[lane], self.part.at[after, rows_of(lane)], self.relay.at[lane])
            self.onward(lane).start()

        self.lanes(step)

    def finish(self, total):
        self.drain()
        add(total, self.part.at[self.x], self.inbox.at[0], self.inbox.at[1])


RING_SUM = [
    pltpu.VMEM((2, HALF, WIDTH), jnp.bfloat16),
    pltpu.VMEM((2, HALF, WIDTH), jnp.bfloat16),
    pltpu.VMEM((2, ROWS, WIDTH), jnp.bfloat16),
]


class ChainSum:
    def __init__(self, part, out, inbox, send, recv, base):
        self.refs = (part, out, inbox, send, recv, base)
        self.x, self.z = place()

    def copy(self, step, lane, own=False):
        part, out, inbox, send, recv, base = self.refs
        source = part.at[self.slot(step, lane)] if own else out.at[lane, step]
        target = device(self.x, self.z + 1 - 2 * lane)
        return remote(source, inbox.at[lane, step], send, recv, base + step + 3 * lane, target)

    def slot(self, step, lane):
        return jnp.where(lane == 0, SIDE - 1 - step, step)

    def sends(self, step, lane):
        slot = self.slot(step, lane)
        return ((lane == 0) & (self.z < slot)) | ((lane == 1) & (self.z > slot))

    def fed(self, lane):
        return ((lane == 0) & (self.z > 0)) | ((lane == 1) & (self.z < SIDE - 1))

    def start(self):
        @pl.loop(0, 2 * (SIDE - 1))
        def _(i):
            step, lane = lax.div(i, 2), lax.rem(i, 2)

            @pl.when(self.sends(step, lane) & jnp.logical_not(self.fed(lane)))
            def _():
                self.copy(step, lane, True).start()

    def forward(self, step):
        part, out, inbox = self.refs[:3]

        @pl.loop(0, 2)
        def _(i):
            lane = lax.rem(i + lax.div(self.z, 2), 2)

            @pl.when(self.sends(step, lane) & self.fed(lane))
            def _():
                self.copy(step, lane).wait_recv()
                add(out.at[lane, step], part.at[self.slot(step, lane)], inbox.at[lane, step])
                self.copy(step, lane).start()

    def finish(self, total):
        part, out, inbox = self.refs[:3]
        add(total, part.at[self.z])

        @pl.loop(0, 2)
        def _(lane):
            step = jnp.where(lane == 0, SIDE - 1 - self.z, self.z)

            @pl.when(self.fed(lane))
            def _():
                self.copy(step, lane).wait_recv()
                add(total, total, inbox.at[lane, step])

        @pl.loop(0, 2 * (SIDE - 1))
        def _(i):
            step, lane = lax.div(i, 2), lax.rem(i, 2)

            @pl.when(self.sends(step, lane))
            def _():
                self.copy(step, lane).wait_send()


CHAIN_SUM = [
    pltpu.VMEM((2, 2, SIDE - 1, HALF, WIDTH), jnp.bfloat16),
    pltpu.VMEM((2, 2, SIDE - 1, HALF, WIDTH), jnp.bfloat16),
]


def semaphores(count):
    return [pltpu.SemaphoreType.DMA((count,)), pltpu.SemaphoreType.DMA((count,))]


def call(kernel, name, number, out, scratch, flops=0, specs=None):
    def run(*args):
        return pl.pallas_call(
            kernel,
            out_shape=out,
            in_specs=specs or [VMEM] * len(args),
            out_specs=jax.tree.map(lambda _: VMEM, out),
            scratch_shapes=scratch,
            compiler_params=pltpu.CompilerParams(
                collective_id=number,
                has_side_effects=number is not None,
                vmem_limit_bytes=48 * 2**20,
            ),
            cost_estimate=pl.CostEstimate(flops=flops, bytes_accessed=2**25, transcendentals=0),
            name=name,
        )(*args)

    return run


def bf16(*shape):
    return jax.ShapeDtypeStruct(shape, jnp.bfloat16)


def f32(*shape):
    return jax.ShapeDtypeStruct(shape, jnp.float32)


def keep(src, dst, sem):
    copy = pltpu.make_async_copy(src, dst, sem)
    copy.start()
    return copy


def chain_gathers(src, dst, send, recv, base):
    return [
        ChainGather(src.at[rows], dst.at[:, rows], send, recv, base + 6 * part)
        for part, rows in enumerate(HALVES)
    ]


def gather(pair, images, texts, send, recv, local):
    x, z = place()
    greet((1, 3))
    chains = chain_gathers(pair.at[1], texts, send, recv, 6)
    ring = RingGather(pair.at[0], images, send, recv, 0)
    for chain in chains:
        chain.start()
    ring.start()
    kept = [keep(pair.at[0], images.at[x], local.at[0]), keep(pair.at[1], texts.at[z], local.at[1])]
    ring.forward()
    for step in range(SIDE - 1):
        for chain in chains:
            chain.forward(step)
    ring.finish()
    for chain in chains:
        chain.finish()
    for copy in kept:
        copy.wait()


def core(
    scalars,
    own_images,
    own_texts,
    one_images,
    one_texts,
    pair,
    positive,
    image_sum,
    text_sum,
    *scratch,
):
    two_images, two_texts, part_image, part_text, ga, gt, places = scratch[:7]
    relay, out, inbox, chain_out, chain_in, send, recv, local = scratch[7:]
    x, z = place()
    scale = scalars[0]
    bias = scalars[1]
    greet((1, 2, 3))
    chains = chain_gathers(pair.at[1], two_texts, send, recv, 0)
    ring = RingGather(pair.at[0], two_images, send, recv, 12)

    def hint(k):
        return remote(positive, places.at[x], send, recv, 17 + k, device(x + k, z))

    @pl.loop(1, SIDE)
    def _(k):
        hint(k).start()

    ring.start()
    for chain in chains:
        chain.start()
    kept = [
        keep(positive, places.at[x], local.at[0]),
        keep(pair.at[0], two_images.at[x], local.at[1]),
        keep(pair.at[1], two_texts.at[z], local.at[2]),
    ]

    def weights(images, texts):
        prod = lax.dot_general(
            images[...].reshape(TILE, WIDTH),
            texts[...].reshape(TILE, WIDTH),
            (((1,), (1,)), ((), ())),
            preferred_element_type=jnp.float32,
        )
        return 0.5 * jnp.tanh(0.5 * (scale * prod + bias)) + 0.5

    def image_term(grad, texts):
        right = texts[...].reshape(TILE, WIDTH)
        return jnp.dot(grad, right, preferred_element_type=jnp.float32)

    def text_term(grad, images):
        right = images[...].reshape(TILE, WIDTH)
        return lax.dot_general(
            grad, right, (((0,), (0,)), ((), ())), preferred_element_type=jnp.float32
        )

    def marked():
        lanes = lax.broadcasted_iota(jnp.int32, (ROWS, ROWS), 1)
        diagonal = lax.broadcasted_iota(jnp.int32, (ROWS, ROWS), 0) == lanes
        index = (lax.broadcasted_iota(jnp.int32, (ROWS, TILE), 1) + x * TILE).astype(jnp.float32)
        marks = []
        for slot in range(SIDE):
            spots = jnp.broadcast_to(places[slot].astype(jnp.float32), (ROWS, ROWS))
            spot = jnp.sum(jnp.where(diagonal, spots, 0.0), axis=1, keepdims=True)
            marks.append(jnp.where(index == spot, 1.0, 0.0))
        return jnp.concatenate(marks, axis=0)

    grad = weights(one_images, own_texts).astype(jnp.bfloat16)
    gt[...] = text_term(grad, one_images)
    ring.forward()
    grad = weights(own_images, one_texts).astype(jnp.bfloat16)
    ga[...] = image_term(grad, one_texts)
    for chain in chains:
        chain.forward(0)

    @pl.loop(1, SIDE)
    def _(k):
        hint(k).wait()

    for copy in kept:
        copy.wait()
    grad = (weights(own_images, own_texts) - marked()).astype(jnp.bfloat16)
    gt[...] += text_term(grad, own_images)
    ga[...] += image_term(grad, own_texts)
    ring.finish()
    chains[0].forward(1)
    grad = weights(two_images, own_texts).astype(jnp.bfloat16)
    total = gt[...] + text_term(grad, two_images)
    part_text[...] = total.astype(jnp.bfloat16).reshape(SIDE, ROWS, WIDTH)
    chains[1].forward(1)
    sums = [
        ChainSum(part_text.at[:, rows], chain_out.at[k], chain_in.at[k], send, recv, 21 + 6 * k)
        for k, rows in enumerate(HALVES)
    ]
    for total in sums:
        total.start()
    for chain in chains:
        chain.forward(2)
        chain.finish()
    grad = weights(own_images, two_texts).astype(jnp.bfloat16)
    total = scale * (ga[...] + image_term(grad, two_texts))
    part_image[...] = total.astype(jnp.bfloat16).reshape(SIDE, ROWS, WIDTH)
    ring = RingSum(part_image, relay, out, inbox, send, recv, 33)
    ring.start()
    for total in sums:
        total.forward(0)
    ring.forward()
    for step in (1, 2):
        for total in sums:
            total.forward(step)
    ring.finish(image_sum)
    for total, rows in zip(sums, HALVES):
        total.finish(text_sum.at[rows])


def exchange(value, mask, beside):
    count = lax.axis_size("blk")

    def branch(m):
        pairs = [(source, source ^ m) for source in range(count)]
        return lambda v, w: (lax.ppermute(v, "blk", pairs), beside(w))

    branches = [branch(m) for m in range(1, count)]
    return lambda other: lax.switch(mask - 1, branches, value, other)


def unit_rows(x):
    xf = x.astype(jnp.float32)
    norm = jnp.sqrt(jnp.sum(xf * xf, axis=-1, keepdims=True) + 1e-06)
    return (xf / norm, norm)


def prepare(image, text, pair, raw, local):
    kept = [keep(source, raw.at[slot], local.at[slot]) for slot, source in enumerate((image, text))]
    for slot in range(2):
        kept[slot].wait()
        pair[slot] = unit_rows(raw[slot])[0].astype(jnp.bfloat16)


def norm_backward(grad, value):
    unit, norm = unit_rows(value)
    return ((grad - unit * jnp.sum(unit * grad, axis=-1, keepdims=True)) / norm).astype(jnp.bfloat16)


def conclude(scalars, image, text, image_sum, text_sum, grad_image, grad_text):
    grad_image[...] = norm_backward(image_sum[...], image[...])
    grad_text[...] = norm_backward(scalars[0] * text_sum[...], text[...])


def shards(image, text, positive, plan, logit_scale, logit_bias):
    masks = plan[:, 0]
    scalars = jnp.concatenate([logit_scale, logit_bias])
    shard = bf16(ROWS, WIDTH)
    wide = f32(ROWS, WIDTH)
    stack = bf16(SIDE, ROWS, WIDTH)
    room = pltpu.VMEM((SIDE, ROWS, WIDTH), jnp.bfloat16)
    total = pltpu.VMEM((TILE, WIDTH), jnp.float32)

    anywhere = pl.BlockSpec(memory_space=pl.ANY)
    own = call(
        prepare,
        "prepare",
        None,
        bf16(2, ROWS, WIDTH),
        [pltpu.VMEM((2, ROWS, WIDTH), jnp.bfloat16), pltpu.SemaphoreType.DMA((2,))],
        specs=[anywhere, anywhere],
    )(image, text)
    scratch = [*semaphores(18), pltpu.SemaphoreType.DMA((2,))]
    beside = call(gather, "gather", 0, (stack, stack), scratch)
    one, (own_images, own_texts) = exchange(own, masks[0], beside)(own)
    two, (one_images, one_texts) = exchange(own, masks[1], beside)(one)
    middle = call(
        core,
        "core",
        1,
        (wide, wide),
        [
            *[room] * 4,
            *[total] * 2,
            pltpu.VMEM((SIDE, 1, ROWS), jnp.int32),
            *RING_SUM,
            *CHAIN_SUM,
            *semaphores(39),
            pltpu.SemaphoreType.DMA((3,)),
        ],
        flops=24 * TILE * TILE * WIDTH,
        specs=[SMEM] + [VMEM] * 6,
    )
    image_sum, text_sum = middle(
        scalars, own_images, own_texts, one_images, one_texts, two, positive.reshape(1, ROWS)
    )
    last = call(conclude, "conclude", None, (shard, shard), [], specs=[SMEM] + [VMEM] * 4)
    return last(scalars, image, text, image_sum, text_sum)


def solution(mesh):
    placed = (P(("blk", "row"), None), P(("blk", "row"), None), P(("blk", "row")), P(), P(), P())
    return jax.shard_map(
        shards,
        mesh=mesh,
        in_specs=placed,
        out_specs=(P(("blk", "row"), None), P(("blk", "row"), None)),
        check_vma=False,
    )
```

```python
import jax
import jax.numpy as jnp
from jax import lax
from jax.experimental import pallas as pl
from jax.experimental.pallas import tpu as pltpu
from jax.sharding import PartitionSpec as P

MESH = pl.DeviceIdType.MESH
VMEM = pl.BlockSpec(memory_space=pltpu.VMEM)
SMEM = pl.BlockSpec(memory_space=pltpu.SMEM)
SIDE = 4
ROWS = 96
HALF = 48
TILE = SIDE * ROWS
WIDTH = 1152


def place():
    row = lax.axis_index("row")
    return lax.div(row, SIDE), lax.rem(row, SIDE)


def device(x, z):
    return {"row": lax.rem(x, SIDE) * SIDE + z}


def remote(src, dst, send, recv, index, target):
    return pltpu.make_async_remote_copy(
        src_ref=src,
        dst_ref=dst,
        send_sem=send.at[index],
        recv_sem=recv.at[index],
        device_id=target,
        device_id_type=MESH,
    )


def greet(offsets):
    x, z = place()
    barrier = pltpu.get_barrier_semaphore()

    def signal(target):
        pl.semaphore_signal(barrier, inc=1, device_id=target, device_id_type=MESH)

    for offset in offsets:
        signal(device(x + offset, z))

    @pl.when(z < SIDE - 1)
    def _():
        signal(device(x, z + 1))

    @pl.when(z > 0)
    def _():
        signal(device(x, z - 1))

    ends = jnp.where(z < SIDE - 1, 1, 0) + jnp.where(z > 0, 1, 0)
    pl.semaphore_wait(barrier, len(offsets) + ends)


HALVES = (pl.ds(0, HALF), pl.ds(HALF, HALF))


def rows_of(lane):
    return pl.ds(pl.multiple_of(lane * HALF, 16), HALF)


class Ring:
    def lanes(self, step):
        @pl.loop(0, 2)
        def _(lane):
            step(lane)

    def ends(self, lane):
        sign = 1 - 2 * lane
        after = lax.rem(self.x + sign + SIDE, SIDE)
        before = lax.rem(self.x - sign + SIDE, SIDE)
        return after, before, device(after, self.z)

    def start(self):
        self.lanes(lambda lane: self.first(lane).start())
        self.lanes(lambda lane: self.second(lane).start())

    def drain(self):
        def step(lane):
            self.second(lane).wait_recv()
            self.onward(lane).wait_recv()
            for copy in (self.first, self.second, self.onward):
                copy(lane).wait_send()

        self.lanes(step)


class RingGather(Ring):
    def __init__(self, src, dst, send, recv, base):
        self.src, self.dst, self.sems = src, dst, (send, recv)
        self.base = base
        self.x, self.z = place()

    def copy(self, source, slot, rows, index, target):
        return remote(source.at[rows], self.dst.at[slot, rows], *self.sems, self.base + index, target)

    def first(self, lane):
        return self.copy(self.src, self.x, rows_of(lane), lane, self.ends(lane)[2])

    def second(self, lane):
        return self.copy(self.src, self.x, rows_of(1 - lane), 2 + lane, self.ends(lane)[2])

    def onward(self, lane):
        _, before, target = self.ends(lane)
        return self.copy(self.dst.at[before], before, rows_of(lane), 4 + lane, target)

    def forward(self):
        def step(lane):
            self.first(lane).wait_recv()
            self.onward(lane).start()

        self.lanes(step)

    def finish(self):
        self.drain()


class ChainGather:
    def __init__(self, src, dst, send, recv, base):
        self.refs = (src, dst, send, recv, base)
        self.x, self.z = place()

    def copy(self, step, lane, own=False):
        src, dst, send, recv, base = self.refs
        sign = 1 - 2 * lane
        slot = self.z - sign * step
        source = src if own else dst.at[slot]
        target = device(self.x, self.z + sign)
        return remote(source, dst.at[slot], send, recv, base + step + 3 * lane, target)

    def sends(self, step, lane):
        edge = self.z + 1 - 2 * lane
        first = self.z - (1 - 2 * lane) * step
        return (first >= 0) & (first < SIDE) & (edge >= 0) & (edge < SIDE) & (step < SIDE - 1)

    def gets(self, step, lane):
        first = self.z - (1 - 2 * lane) * (step + 1)
        return (first >= 0) & (first < SIDE)

    def start(self):
        @pl.loop(0, 2)
        def _(lane):
            @pl.when(self.sends(0, lane))
            def _():
                self.copy(0, lane, True).start()

    def forward(self, step):
        @pl.loop(0, 2)
        def _(lane):
            @pl.when(self.gets(step, lane))
            def _():
                self.copy(step, lane).wait_recv()

            @pl.when(self.sends(step + 1, lane))
            def _():
                self.copy(step + 1, lane).start()

    def finish(self):
        @pl.loop(0, 2 * (SIDE - 1))
        def _(i):
            step, lane = lax.div(i, 2), lax.rem(i, 2)

            @pl.when(self.sends(step, lane))
            def _():
                self.copy(step, lane).wait_send()


def add(out, *terms):
    @pl.loop(0, out.shape[0] // 16)
    def _(i):
        rows = pl.ds(pl.multiple_of(i * 16, 16), 16)
        total = terms[0][rows].astype(jnp.float32)
        for term in terms[1:]:
            total = total + term[rows].astype(jnp.float32)
        out[rows] = total.astype(out.dtype)


class RingSum(Ring):
    def __init__(self, part, relay, out, inbox, send, recv, base):
        self.x, self.z = place()
        self.part, self.relay, self.out, self.inbox = part, relay, out, inbox
        self.sems, self.base = (send, recv), base

    def first(self, lane):
        across = lax.rem(self.x + 2, SIDE)
        source = self.part.at[across, rows_of(lane)]
        return remote(source, self.relay.at[lane], *self.sems, self.base + lane, self.ends(lane)[2])

    def second(self, lane):
        after, _, target = self.ends(lane)
        rows = rows_of(1 - lane)
        source, into = self.part.at[after, rows], self.inbox.at[lane, rows]
        return remote(source, into, *self.sems, self.base + 2 + lane, target)

    def onward(self, lane):
        into = self.inbox.at[lane, rows_of(lane)]
        index, target = self.base + 4 + lane, self.ends(lane)[2]
        return remote(self.out.at[lane], into, *self.sems, index, target)

    def forward(self):
        def step(lane):
            self.first(lane).wait_recv()
            after = self.ends(lane)[0]
            add(self.out.at[lane], self.part.at[after, rows_of(lane)], self.relay.at[lane])
            self.onward(lane).start()

        self.lanes(step)

    def finish(self, total):
        self.drain()
        add(total, self.part.at[self.x], self.inbox.at[0], self.inbox.at[1])


RING_SUM = [
    pltpu.VMEM((2, HALF, WIDTH), jnp.bfloat16),
    pltpu.VMEM((2, HALF, WIDTH), jnp.bfloat16),
    pltpu.VMEM((2, ROWS, WIDTH), jnp.bfloat16),
]


class ChainSum:
    def __init__(self, part, out, inbox, send, recv, base):
        self.refs = (part, out, inbox, send, recv, base)
        self.x, self.z = place()

    def copy(self, step, lane, own=False):
        part, out, inbox, send, recv, base = self.refs
        source = part.at[self.slot(step, lane)] if own else out.at[lane, step]
        target = device(self.x, self.z + 1 - 2 * lane)
        return remote(source, inbox.at[lane, step], send, recv, base + step + 3 * lane, target)

    def slot(self, step, lane):
        return jnp.where(lane == 0, SIDE - 1 - step, step)

    def sends(self, step, lane):
        slot = self.slot(step, lane)
        return ((lane == 0) & (self.z < slot)) | ((lane == 1) & (self.z > slot))

    def fed(self, lane):
        return ((lane == 0) & (self.z > 0)) | ((lane == 1) & (self.z < SIDE - 1))

    def start(self):
        @pl.loop(0, 2 * (SIDE - 1))
        def _(i):
            step, lane = lax.div(i, 2), lax.rem(i, 2)

            @pl.when(self.sends(step, lane) & jnp.logical_not(self.fed(lane)))
            def _():
                self.copy(step, lane, True).start()

    def forward(self, step):
        part, out, inbox = self.refs[:3]

        @pl.loop(0, 2)
        def _(i):
            lane = lax.rem(i + lax.div(self.z, 2), 2)

            @pl.when(self.sends(step, lane) & self.fed(lane))
            def _():
                self.copy(step, lane).wait_recv()
                add(out.at[lane, step], part.at[self.slot(step, lane)], inbox.at[lane, step])
                self.copy(step, lane).start()

    def finish(self, total):
        part, out, inbox = self.refs[:3]
        add(total, part.at[self.z])

        @pl.loop(0, 2)
        def _(lane):
            step = jnp.where(lane == 0, SIDE - 1 - self.z, self.z)

            @pl.when(self.fed(lane))
            def _():
                self.copy(step, lane).wait_recv()
                add(total, total, inbox.at[lane, step])

        @pl.loop(0, 2 * (SIDE - 1))
        def _(i):
            step, lane = lax.div(i, 2), lax.rem(i, 2)

            @pl.when(self.sends(step, lane))
            def _():
                self.copy(step, lane).wait_send()


CHAIN_SUM = [
    pltpu.VMEM((2, 2, SIDE - 1, HALF, WIDTH), jnp.bfloat16),
    pltpu.VMEM((2, 2, SIDE - 1, HALF, WIDTH), jnp.bfloat16),
]


def semaphores(count):
    return [pltpu.SemaphoreType.DMA((count,)), pltpu.SemaphoreType.DMA((count,))]


def call(kernel, name, number, out, scratch, flops=0, specs=None):
    def run(*args):
        return pl.pallas_call(
            kernel,
            out_shape=out,
            in_specs=specs or [VMEM] * len(args),
            out_specs=jax.tree.map(lambda _: VMEM, out),
            scratch_shapes=scratch,
            compiler_params=pltpu.CompilerParams(
                collective_id=number,
                has_side_effects=number is not None,
                vmem_limit_bytes=48 * 2**20,
            ),
            cost_estimate=pl.CostEstimate(flops=flops, bytes_accessed=2**25, transcendentals=0),
            name=name,
        )(*args)

    return run


def bf16(*shape):
    return jax.ShapeDtypeStruct(shape, jnp.bfloat16)


def f32(*shape):
    return jax.ShapeDtypeStruct(shape, jnp.float32)


def keep(src, dst, sem):
    copy = pltpu.make_async_copy(src, dst, sem)
    copy.start()
    return copy


def chain_gathers(src, dst, send, recv, base):
    return [
        ChainGather(src.at[rows], dst.at[:, rows], send, recv, base + 6 * part)
        for part, rows in enumerate(HALVES)
    ]


def gather(pair, images, texts, send, recv, local):
    x, z = place()
    greet((1, 3))
    chains = chain_gathers(pair.at[1], texts, send, recv, 6)
    ring = RingGather(pair.at[0], images, send, recv, 0)
    for chain in chains:
        chain.start()
    ring.start()
    kept = [keep(pair.at[0], images.at[x], local.at[0]), keep(pair.at[1], texts.at[z], local.at[1])]
    ring.forward()
    for step in range(SIDE - 1):
        for chain in chains:
            chain.forward(step)
    ring.finish()
    for chain in chains:
        chain.finish()
    for copy in kept:
        copy.wait()


def core(
    scalars,
    own_images,
    own_texts,
    one_images,
    one_texts,
    pair,
    positive,
    image_sum,
    text_sum,
    *scratch,
):
    two_images, two_texts, part_image, part_text, ga, gt, places = scratch[:7]
    relay, out, inbox, chain_out, chain_in, send, recv, local = scratch[7:]
    x, z = place()
    scale = scalars[0]
    bias = scalars[1]
    greet((1, 2, 3))
    chains = chain_gathers(pair.at[1], two_texts, send, recv, 0)
    ring = RingGather(pair.at[0], two_images, send, recv, 12)

    def hint(k):
        return remote(positive, places.at[x], send, recv, 17 + k, device(x + k, z))

    @pl.loop(1, SIDE)
    def _(k):
        hint(k).start()

    ring.start()
    for chain in chains:
        chain.start()
    kept = [
        keep(positive, places.at[x], local.at[0]),
        keep(pair.at[0], two_images.at[x], local.at[1]),
        keep(pair.at[1], two_texts.at[z], local.at[2]),
    ]

    def weights(images, texts):
        prod = lax.dot_general(
            images[...].reshape(TILE, WIDTH),
            texts[...].reshape(TILE, WIDTH),
            (((1,), (1,)), ((), ())),
            preferred_element_type=jnp.float32,
        )
        return 0.5 * jnp.tanh(0.5 * (scale * prod + bias)) + 0.5

    def image_term(grad, texts):
        right = texts[...].reshape(TILE, WIDTH)
        return jnp.dot(grad, right, preferred_element_type=jnp.float32)

    def text_term(grad, images):
        right = images[...].reshape(TILE, WIDTH)
        return lax.dot_general(
            grad, right, (((0,), (0,)), ((), ())), preferred_element_type=jnp.float32
        )

    def marked():
        lanes = lax.broadcasted_iota(jnp.int32, (ROWS, ROWS), 1)
        diagonal = lax.broadcasted_iota(jnp.int32, (ROWS, ROWS), 0) == lanes
        index = (lax.broadcasted_iota(jnp.int32, (ROWS, TILE), 1) + x * TILE).astype(jnp.float32)
        marks = []
        for slot in range(SIDE):
            spots = jnp.broadcast_to(places[slot].astype(jnp.float32), (ROWS, ROWS))
            spot = jnp.sum(jnp.where(diagonal, spots, 0.0), axis=1, keepdims=True)
            marks.append(jnp.where(index == spot, 1.0, 0.0))
        return jnp.concatenate(marks, axis=0)

    grad = weights(one_images, own_texts).astype(jnp.bfloat16)
    gt[...] = text_term(grad, one_images)
    ring.forward()
    grad = weights(own_images, one_texts).astype(jnp.bfloat16)
    ga[...] = image_term(grad, one_texts)
    for chain in chains:
        chain.forward(0)

    @pl.loop(1, SIDE)
    def _(k):
        hint(k).wait()

    for copy in kept:
        copy.wait()
    grad = (weights(own_images, own_texts) - marked()).astype(jnp.bfloat16)
    gt[...] += text_term(grad, own_images)
    ga[...] += image_term(grad, own_texts)
    ring.finish()
    chains[0].forward(1)
    grad = weights(two_images, own_texts).astype(jnp.bfloat16)
    total = gt[...] + text_term(grad, two_images)
    part_text[...] = total.astype(jnp.bfloat16).reshape(SIDE, ROWS, WIDTH)
    chains[1].forward(1)
    sums = [
        ChainSum(part_text.at[:, rows], chain_out.at[k], chain_in.at[k], send, recv, 21 + 6 * k)
        for k, rows in enumerate(HALVES)
    ]
    for total in sums:
        total.start()
    for chain in chains:
        chain.forward(2)
        chain.finish()
    grad = weights(own_images, two_texts).astype(jnp.bfloat16)
    total = scale * (ga[...] + image_term(grad, two_texts))
    part_image[...] = total.astype(jnp.bfloat16).reshape(SIDE, ROWS, WIDTH)
    ring = RingSum(part_image, relay, out, inbox, send, recv, 33)
    ring.start()
    for total in sums:
        total.forward(0)
    ring.forward()
    for step in (1, 2):
        for total in sums:
            total.forward(step)
    ring.finish(image_sum)
    for total, rows in zip(sums, HALVES):
        total.finish(text_sum.at[rows])


def exchange(value, mask, beside):
    count = lax.axis_size("blk")

    def branch(m):
        pairs = [(source, source ^ m) for source in range(count)]
        return lambda v, w: (lax.ppermute(v, "blk", pairs), beside(w))

    branches = [branch(m) for m in range(1, count)]
    return lambda other: lax.switch(mask - 1, branches, value, other)


def unit_rows(x):
    xf = x.astype(jnp.float32)
    norm = jnp.sqrt(jnp.sum(xf * xf, axis=-1, keepdims=True) + 1e-06)
    return (xf / norm, norm)


def prepare(image, text, pair, raw, local):
    kept = [keep(source, raw.at[slot], local.at[slot]) for slot, source in enumerate((image, text))]
    for slot in range(2):
        kept[slot].wait()
        pair[slot] = unit_rows(raw[slot])[0].astype(jnp.bfloat16)


def norm_backward(grad, value):
    unit, norm = unit_rows(value)
    return ((grad - unit * jnp.sum(unit * grad, axis=-1, keepdims=True)) / norm).astype(jnp.bfloat16)


def conclude(scalars, image, text, image_sum, text_sum, grad_image, grad_text):
    grad_image[...] = norm_backward(image_sum[...], image[...])
    grad_text[...] = norm_backward(scalars[0] * text_sum[...], text[...])


def shards(image, text, positive, plan, logit_scale, logit_bias):
    masks = plan[:, 0]
    scalars = jnp.concatenate([logit_scale, logit_bias])
    shard = bf16(ROWS, WIDTH)
    wide = f32(ROWS, WIDTH)
    stack = bf16(SIDE, ROWS, WIDTH)
    room = pltpu.VMEM((SIDE, ROWS, WIDTH), jnp.bfloat16)
    total = pltpu.VMEM((TILE, WIDTH), jnp.float32)

    anywhere = pl.BlockSpec(memory_space=pl.ANY)
    own = call(
        prepare,
        "prepare",
        None,
        bf16(2, ROWS, WIDTH),
        [pltpu.VMEM((2, ROWS, WIDTH), jnp.bfloat16), pltpu.SemaphoreType.DMA((2,))],
        specs=[anywhere, anywhere],
    )(image, text)
    scratch = [*semaphores(18), pltpu.SemaphoreType.DMA((2,))]
    beside = call(gather, "gather", 0, (stack, stack), scratch)
    one, (own_images, own_texts) = exchange(own, masks[0], beside)(own)
    two, (one_images, one_texts) = exchange(own, masks[1], beside)(one)
    middle = call(
        core,
        "core",
        1,
        (wide, wide),
        [
            *[room] * 4,
            *[total] * 2,
            pltpu.VMEM((SIDE, 1, ROWS), jnp.int32),
            *RING_SUM,
            *CHAIN_SUM,
            *semaphores(39),
            pltpu.SemaphoreType.DMA((3,)),
        ],
        flops=24 * TILE * TILE * WIDTH,
        specs=[SMEM] + [VMEM] * 4 + [anywhere] * 2,
    )
    image_sum, text_sum = middle(
        scalars, own_images, own_texts, one_images, one_texts, two, positive.reshape(1, ROWS)
    )
    last = call(conclude, "conclude", None, (shard, shard), [], specs=[SMEM] + [VMEM] * 4)
    return last(scalars, image, text, image_sum, text_sum)


def solution(mesh):
    placed = (P(("blk", "row"), None), P(("blk", "row"), None), P(("blk", "row")), P(), P(), P())
    return jax.shard_map(
        shards,
        mesh=mesh,
        in_specs=placed,
        out_specs=(P(("blk", "row"), None), P(("blk", "row"), None)),
        check_vma=False,
    )
```
